256 devices in a mesh: mode: 8 (over z_hi, core), space: 32 (over z_lo, y, x).
Axes of the slice: x: 4, y: 4, z: 8 (z_hi: 4, z_lo: 2; z = z_hi * 2 + z_lo), core: 2. Of those that a mesh axis runs over, the one named last changes fastest.
Arguments:
- anomalies: bfloat16 [8, 136, 128, 2048], P('mode', None, 'space'), may hold values from -6 to 6
- vector: float32 [136, 128, 2048], P(None, 'space'), may hold values from -6 to 6
- modes: float32 [16, 136], P('mode'), may hold values from -0.5 to 0.5
- order: int32 [8], replicated, may hold values from 0 to 7, each once
- weights: float32 [8], replicated, may hold values from 0.3 to 3
- diffusivity: float32 [128, 2048], P('space'), may hold values from 0.04 to 0.24
Outputs:
- increment: float32 [136, 128, 2048], P('mode', 'space')
The draws below stay inside these ranges and needn't reach their ends.
Inputs may be any that keep to these rules, and one draw needn't show every extreme that they name: `order`: each member appears once.
All inputs are finite; a program needn't handle non-finite values.
Results may differ from the reference program's by a relative error of at most 0.0003.
Values may be sent and summed in bfloat16 or wider, within the bound.
A program may use at most 128 MiB of HBM per device.

```python
import math
import jax
import jax.numpy as jnp
from jax import lax

LEV = 136
NLON = 2048
DIFF = 4
MODES = 16
MEMBERS = 8
NLAT = 128


def levels(key, extent, shards, low, top_value):
    def one(position, shards_of):
        heights = jax.random.uniform(jax.random.fold_in(jax.random.fold_in(key, 6), position), (shards_of,), jnp.float32, low / len(shards), top_value / len(shards))
        return jnp.repeat(jnp.exp(heights), extent[position] // shards_of).reshape((-1,) + (1,) * (len(extent) - position - 1))

    gain = one(*shards[0])
    for cut in shards[1:]:
        gain = gain * one(*cut)
    return gain


def normal_values(rng, dims, spread, limit, split=(), dtype=jnp.bfloat16):
    entries = spread * jax.random.normal(rng, dims, jnp.float32)
    if split:
        entries = entries * levels(rng, dims, split, -0.22, 0.18)
    return jnp.clip(entries, -limit, limit).astype(dtype)


def setup_inputs(seed: int = 0) -> dict:
    keys = jax.random.split(jax.random.key(seed), 7)
    return {
        "anomalies": normal_values(keys[0], (MEMBERS, LEV, NLAT, NLON), 1.0, 6.0, ((0, 8), (2, 32))),
        "vector": normal_values(keys[1], (LEV, NLAT, NLON), 1.0, 6.0, ((1, 32),), jnp.float32),
        "modes": normal_values(keys[2], (MODES, LEV), LEV ** -0.5, 0.5, ((0, 8),), jnp.float32),
        "order": jax.random.permutation(keys[3], MEMBERS).astype(jnp.int32),
        "weights": jnp.clip(jnp.exp(jax.random.uniform(keys[4], (MEMBERS,), jnp.float32, math.log(0.3), math.log(3.0))), 0.3, 3.0),
        "diffusivity": jnp.clip(0.04 + 0.19999999552965164 * jax.random.uniform(keys[5], (NLAT, NLON), jnp.float32) ** levels(keys[5], (NLAT, NLON), ((0, 32),), -0.2, 0.2), 0.04, 0.24),
    }


def sweep(padded, coeff):
    centre = padded[:, 1:-1]
    here = coeff[1:-1]
    total = centre + 0.5 * (here + coeff[2:]) * (padded[:, 2:] - centre)
    total = total + 0.5 * (here + coeff[:-2]) * (padded[:, :-2] - centre)
    east = jnp.roll(here, -1, axis=1)
    west = jnp.roll(here, 1, axis=1)
    total = total + 0.5 * (here + east) * (jnp.roll(centre, -1, axis=2) - centre)
    total = total + 0.5 * (here + west) * (jnp.roll(centre, 1, axis=2) - centre)
    return total


def contribution(member_field, vector, modes, weight, coeff):
    xf = member_field.astype(jnp.float32)
    product = xf * vector
    projected = jnp.einsum('kl,lan->kan', modes, product, precision=lax.Precision.HIGHEST)
    fields = projected
    for sweep_index in range(DIFF):
        fields = sweep(jnp.pad(fields, ((0, 0), (1, 1), (0, 0))), coeff)
    back = jnp.einsum('kl,kan->lan', modes, fields, precision=lax.Precision.HIGHEST)
    return weight * xf * back


def reference(anomalies, vector, modes, order, weights, diffusivity):
    coeff = jnp.pad(diffusivity, ((1, 1), (0, 0)))

    def step(index, total):
        member = order[index].astype(jnp.int32)
        member_field = lax.dynamic_index_in_dim(anomalies, member, 0, keepdims=False)
        return total + contribution(member_field, vector, modes, weights[index], coeff)

    return lax.fori_loop(0, MEMBERS, step, jnp.zeros(vector.shape, jnp.float32))
```

```python
import jax
import jax.numpy as jnp
from jax import lax
from jax.sharding import PartitionSpec as P

DIFF = 4


def extended(cells, axis, dim, width):
    count = lax.axis_size(axis)
    ends = count - 1
    head = lax.slice_in_dim(cells, 0, width, axis=dim)
    tail = lax.slice_in_dim(cells, cells.shape[dim] - width, cells.shape[dim], axis=dim)
    return jnp.concatenate(
        [
            lax.ppermute(tail, axis, [(i, (i + 1) % count) for i in range(ends)]),
            cells,
            lax.ppermute(head, axis, [((i + 1) % count, i) for i in range(ends)]),
        ],
        axis=dim,
    )


def sweep(padded, coeff):
    centre = padded[:, 1:-1]
    here = coeff[1:-1]
    total = centre + 0.5 * (here + coeff[2:]) * (padded[:, 2:] - centre)
    total = total + 0.5 * (here + coeff[:-2]) * (padded[:, :-2] - centre)
    east = jnp.roll(here, -1, axis=1)
    west = jnp.roll(here, 1, axis=1)
    total = total + 0.5 * (here + east) * (jnp.roll(centre, -1, axis=2) - centre)
    total = total + 0.5 * (here + west) * (jnp.roll(centre, 1, axis=2) - centre)
    return total


def body(anomalies, vector, modes, order, weights, diffusivity):
    rows = diffusivity.shape[0]
    me = lax.axis_index("mode")
    place = lax.axis_index("space")
    last = lax.axis_size("space") - 1
    modes = lax.all_gather(modes, "mode", axis=0, tiled=True)
    weight = jnp.sum(jnp.where(order == me, weights, 0.0))
    coeff = extended(diffusivity, "space", 0, DIFF)
    xf = anomalies[0].astype(jnp.float32)
    projected = jnp.einsum("kl,lan->kan", modes, xf * vector, precision=lax.Precision.HIGHEST)
    fields = extended(projected, "space", 1, DIFF)
    index = jnp.arange(rows + 2 * DIFF)
    inside = ((index >= DIFF) | (place > 0)) & ((index < rows + DIFF) | (place < last))
    for done in range(1, DIFF + 1):
        stop = rows + 2 * DIFF - done
        fields = sweep(fields, coeff[done - 1 : stop + 1])
        fields = jnp.where(inside[done:stop][None, :, None], fields, 0.0)
    back = jnp.einsum("kl,kan->lan", modes, fields, precision=lax.Precision.HIGHEST)
    return lax.psum_scatter(weight * xf * back, "mode", scatter_dimension=0, tiled=True)


def solution(mesh):
    return jax.shard_map(
        body,
        mesh=mesh,
        in_specs=(
            P("mode", None, "space", None),
            P(None, "space", None),
            P("mode", None),
            P(),
            P(),
            P("space", None),
        ),
        out_specs=P("mode", "space", None),
        check_vma=False,
    )
```

```python
import jax
import jax.numpy as jnp
from jax import lax
from jax.experimental import pallas as pl
from jax.experimental.pallas import tpu as pltpu
from jax.sharding import PartitionSpec as P

LEV, NLON, DIFF, MODES, ROWS = 136, 2048, 4, 16, 4
GROUPS = 8
GLEV = LEV // GROUPS
TILES = NLON // 128
CHUNKS = 4
SUB = TILES * ROWS // CHUNKS
WIDE = NLON // CHUNKS
PADDED = NLON + 256
EXT = ROWS + 2 * DIFF
HALF = (GLEV + 1) // 2
MSGS = CHUNKS + 1
TINY = 1e-33
F32, BF16, I16 = jnp.float32, jnp.bfloat16, jnp.int16


def split(a):
    hi = a.astype(BF16)
    return hi, (a - hi.astype(F32)).astype(BF16)


def pack(a, top):
    return jnp.round(a * (32767.0 / top)).astype(I16)


def kernel(x_hbm, v_hbm, modes_hbm, order_ref, weights_ref, diff_hbm, out_ref,
           xs, vs, mine, nu, mall, nuext, phi, plo, spread, pick, fwd, bwd, field, coef, loc, lcat,
           hq, hsc, hqr, hscr, sib, sibr, own, zq1, zs1, zq1r, zs1r, zqa, zqb, zs2, zqar, zqbr, zs2r,
           lsem, m_s, m_r, d_s, d_r, hq_s, hq_r, hs_s, hs_r, sb_s, sb_r,
           z1_s, z1_r, t1_s, t1_r, z2_s, z2_r, t2_s, t2_r):
    me = lax.axis_index("mode")
    place = lax.axis_index("space")
    ring, core = me // 2, me % 2
    has_prev = place > 0
    has_next = place < lax.axis_size("space") - 1
    right = {"mode": ((ring + 1) % 4) * 2 + core}
    left = {"mode": ((ring + 3) % 4) * 2 + core}
    partner = {"mode": ring * 2 + 1 - core}
    before, after = {"space": place - 1}, {"space": place + 1}

    def remote(src, dst, ss, rs, dev):
        return pltpu.make_async_remote_copy(
            src_ref=src, dst_ref=dst, send_sem=ss, recv_sem=rs, device_id=dev,
            device_id_type=pl.DeviceIdType.MESH)

    def chunk_rows(n):
        return pl.ds(pl.multiple_of(n * SUB, SUB), SUB)

    get_modes = pltpu.make_async_copy(modes_hbm, mine, lsem.at[0])
    get_nu = pltpu.make_async_copy(diff_hbm, nu, lsem.at[1])

    def get_x(n):
        return pltpu.make_async_copy(x_hbm.at[:, chunk_rows(n)], xs.at[:, chunk_rows(n)], lsem.at[2 + n])

    def get_v(n):
        return pltpu.make_async_copy(v_hbm.at[:, chunk_rows(n)], vs.at[:, chunk_rows(n)], lsem.at[2 + CHUNKS + n])

    get_modes.start()
    get_nu.start()
    for n in range(CHUNKS):
        get_x(n).start()
        get_v(n).start()

    barrier = pltpu.get_barrier_semaphore()

    def greet(dev):
        pl.semaphore_signal(barrier, inc=1, device_id=dev, device_id_type=pl.DeviceIdType.MESH)

    for j in range(1, GROUPS):
        greet({"mode": (me + j) % GROUPS})
    pl.when(has_prev)(lambda: greet(before))
    pl.when(has_next)(lambda: greet(after))

    lane_level = lax.broadcasted_iota(jnp.int32, (256, LEV * 8), 1) >> 3
    spread[...] = jnp.where(lane_level == lax.broadcasted_iota(jnp.int32, (256, LEV * 8), 0), 1.0, 0.0).astype(BF16)
    for i in range(GROUPS):
        c = 1 - core if i < 4 else core
        group = ((ring + i) % 4) * 2 + c
        level = group * GLEV + (lax.broadcasted_iota(jnp.int32, (LEV, 256), 0) >> 3)
        pick[i // 4, (i % 4) * LEV : (i % 4 + 1) * LEV, :] = jnp.where(
            lax.broadcasted_iota(jnp.int32, (LEV, 256), 1) == level, 1.0, 0.0).astype(BF16)

    get_modes.wait()
    which = lax.broadcasted_iota(jnp.int32, (MODES, LEV), 0) - 2 * me
    block = jnp.where(which == 0, mine[0:1, :], jnp.where(which == 1, mine[1:2, :], 0.0))
    mall[0] = jnp.concatenate([block, jnp.zeros((MODES, 256 - LEV), F32)], axis=1)
    get_nu.wait()

    def products(n):
        get_x(n).wait()
        get_v(n).wait()

        def part(b, carry):
            lev = pl.ds(b * 8, 8)
            p = xs[lev, chunk_rows(n), :].astype(F32) * vs[lev, chunk_rows(n), :]
            for h in range(2):
                hi, lo = split(p[:, 8 * h : 8 * h + 8, :].reshape(64, 128))
                at = pl.ds(pl.multiple_of(b * 64, 64), 64)
                phi[n, at, 128 * h : 128 * h + 128] = hi
                plo[n, at, 128 * h : 128 * h + 128] = lo
            return carry

        lax.fori_loop(0, LEV // 8, part, 0)

    products(0)
    pl.semaphore_wait(barrier, GROUPS - 1 + has_prev.astype(jnp.int32) + has_next.astype(jnp.int32))

    def send_modes(j):
        return remote(mall.at[0], mall.at[j], m_s.at[j], m_r.at[j], {"mode": (me + j) % GROUPS})

    for j in range(1, GROUPS):
        send_modes(j).start()
    nu_up = remote(nu, nuext.at[0], d_s.at[0], d_r.at[0], after)
    nu_down = remote(nu, nuext.at[1], d_s.at[1], d_r.at[1], before)
    pl.when(has_next)(lambda: nu_up.start())
    pl.when(has_prev)(lambda: nu_down.start())

    for n in range(1, CHUNKS):
        products(n)

    for j in range(1, GROUPS):
        send_modes(j).wait_recv()
    modes = mall[0]
    for j in range(1, GROUPS):
        modes = modes + mall[j]
    modes_hi, modes_lo = split(modes)

    both = jnp.dot(jnp.concatenate([modes_hi, modes_lo], axis=0), spread[...], preferred_element_type=F32)
    sub = lax.broadcasted_iota(jnp.int32, (MODES, LEV * 8), 1) & 7
    for half in range(2):
        rows = both[half * MODES : (half + 1) * MODES]
        for q in range(8):
            fwd[half * 128 + q * MODES : half * 128 + (q + 1) * MODES, :] = jnp.where(sub == q, rows, 0.0).astype(BF16)

    def project(n):
        main = jnp.dot(fwd[...], phi[n], preferred_element_type=F32)
        rest = jnp.dot(fwd[0:128, :], plo[n], preferred_element_type=F32)
        total = main[0:128] + main[128:256] + rest
        for par in range(2):
            for r in range(ROWS):
                for h in range(2):
                    at = (1 + 4 * n + 2 * h + par) * 128
                    q = (par * ROWS + r) * MODES
                    field[DIFF + r, :, at : at + 128] = total[q : q + MODES, h * 128 : h * 128 + 128]

    for n in range(CHUNKS):
        project(n)
    field[DIFF : DIFF + ROWS, :, 0:128] = field[DIFF : DIFF + ROWS, :, NLON : NLON + 128]
    field[DIFF : DIFF + ROWS, :, NLON + 128 : PADDED] = field[DIFF : DIFF + ROWS, :, 128:256]

    def halo_lanes(i):
        if isinstance(i, int) and i == 0:
            return pl.ds(0, 256)
        return pl.ds(pl.multiple_of(i * WIDE - WIDE + 256, 128), WIDE)

    def halo(i, way):
        lanes = halo_lanes(i)
        dev = after if way == 0 else before
        return (remote(hq.at[:, :, lanes], hqr.at[way, :, :, lanes], hq_s.at[way, i], hq_r.at[way, i], dev),
                remote(hsc.at[:, lanes], hscr.at[way, :, lanes], hs_s.at[way, i], hs_r.at[way, i], dev))

    def each(copies, what):
        for copy in copies:
            getattr(copy, what)()

    for i in range(MSGS):
        lanes = halo_lanes(i)
        u = field[DIFF : DIFF + ROWS, :, lanes]
        top = jnp.maximum(jnp.max(jnp.max(jnp.abs(u), axis=0), axis=0, keepdims=True), TINY)
        hsc[:, lanes] = top * (1.0 / 32767.0)
        hq[:, :, lanes] = pack(u, top[None])
        pl.when(has_next)(lambda: each(halo(i, 0), "start"))
        pl.when(has_prev)(lambda: each(halo(i, 1), "start"))

    rep_hi = jnp.concatenate([modes_hi] * 8, axis=0)
    rep_lo = jnp.concatenate([modes_lo] * 8, axis=0)
    same = (lax.broadcasted_iota(jnp.int32, (4 * LEV, 128), 0) & 7) == (lax.broadcasted_iota(jnp.int32, (4 * LEV, 128), 1) >> 4)
    last = (((1,), (1,)), ((), ()))
    for part in range(2):
        hi = lax.dot_general(pick[part], rep_hi, last, preferred_element_type=F32)
        lo = lax.dot_general(pick[part], rep_lo, last, preferred_element_type=F32)
        hi = jnp.where(same, hi, 0.0).astype(BF16)
        bwd[part, :, 0:128] = hi
        bwd[part, :, 128:256] = hi
        bwd[part, :, 256:384] = jnp.where(same, lo, 0.0).astype(BF16)

    @pl.when(has_prev)
    def _():
        nu_up.wait_recv()

    @pl.when(has_next)
    def _():
        nu_down.wait_recv()

    @pl.when(jnp.logical_not(has_prev))
    def _():
        nuext[0] = jnp.zeros((ROWS, NLON), F32)
        field[0:DIFF] = jnp.zeros((DIFF, MODES, PADDED), F32)

    @pl.when(jnp.logical_not(has_next))
    def _():
        nuext[1] = jnp.zeros((ROWS, NLON), F32)
        field[DIFF + ROWS : EXT] = jnp.zeros((DIFF, MODES, PADDED), F32)

    def nu_row(a):
        src = nuext[0] if a < DIFF else nu[...] if a < DIFF + ROWS else nuext[1]
        r = a % ROWS
        return jnp.broadcast_to(src[r : r + 1, :], (8, NLON))

    top_mask, low_mask = has_prev.astype(F32), has_next.astype(F32)
    for a in range(1, EXT - 1):
        here = nu_row(a)
        mask = top_mask if a < DIFF else low_mask if a >= DIFF + ROWS else None
        arms = [0.5 * (here + other) for other in (
            nu_row(a - 1), nu_row(a + 1), pltpu.roll(here, NLON - 1, 1), pltpu.roll(here, 1, 1))]
        arms.append(1.0 - (arms[0] + arms[1] + arms[2] + arms[3]))
        for c, arm in enumerate(arms):
            if mask is not None:
                arm = arm * mask
            coef[c, a - 1, :, 128 : NLON + 128] = arm
            coef[c, a - 1, :, 0:128] = arm[:, NLON - 128 : NLON]
            coef[c, a - 1, :, NLON + 128 : PADDED] = arm[:, 0:128]

    weight = jnp.float32(0.0)
    for s in range(GROUPS):
        weight = weight + jnp.where(order_ref[s] == me, weights_ref[s], 0.0)

    def take_halo(i):
        lanes = halo_lanes(i)

        @pl.when(has_prev)
        def _():
            each(halo(i, 0), "wait_recv")
            field[0:DIFF, :, lanes] = hqr[0, :, :, lanes].astype(F32) * hscr[0, :, lanes][None]

        @pl.when(has_next)
        def _():
            each(halo(i, 1), "wait_recv")
            field[DIFF + ROWS : EXT, :, lanes] = hqr[1, :, :, lanes].astype(F32) * hscr[1, :, lanes][None]

    window = WIDE + 256

    def diffuse(n):
        lanes = pl.ds(pl.multiple_of(n * WIDE, 128), window)
        for kh in range(2):
            u = [field[a, kh * 8 : kh * 8 + 8, lanes] for a in range(EXT)]
            for s in range(1, DIFF + 1):
                new = []
                for a in range(s, EXT - s):
                    c, up, down = u[a - s + 1], u[a - s], u[a - s + 2]
                    new.append(
                        coef[4, a - 1, :, lanes] * c
                        + coef[0, a - 1, :, lanes] * up
                        + coef[1, a - 1, :, lanes] * down
                        + coef[2, a - 1, :, lanes] * pltpu.roll(c, window - 1, 1)
                        + coef[3, a - 1, :, lanes] * pltpu.roll(c, 1, 1))
                u = new
            for r in range(ROWS):
                loc[r, kh * 8 : kh * 8 + 8, :] = weight * u[r][:, 128 : 128 + WIDE]
        for par in range(2):
            for r in range(ROWS):
                q = (par * ROWS + r) * MODES
                for h in range(2):
                    t = (2 * h + par) * 128
                    hi, lo = split(loc[r, :, t : t + 128])
                    cols = slice(h * 128, h * 128 + 128)
                    lcat[q : q + MODES, cols] = hi
                    lcat[128 + q : 128 + q + MODES, cols] = lo
                    lcat[256 + q : 256 + q + MODES, cols] = hi

    def backward(n, part, dst):
        back = jnp.dot(bwd[part], lcat[...], preferred_element_type=F32)
        c = core if part else 1 - core
        for i in range(4):
            group = ((ring + i) % 4) * 2 + c
            xg = xs[pl.ds(group * GLEV, GLEV), chunk_rows(n), :].astype(F32)
            for h in range(2):
                b = back[i * LEV : (i + 1) * LEV, h * 128 : h * 128 + 128].reshape(GLEV, 8, 128)
                dst[n, i, :, 8 * h : 8 * h + 8, :] = xg[:, 8 * h : 8 * h + 8, :] * b

    def share(n):
        return remote(sib.at[n], sibr.at[n], sb_s.at[n], sb_r.at[n], partner)

    def first(n, way):
        dev = right if way == 0 else left
        return (remote(zq1.at[n, way], zq1r.at[n, way], z1_s.at[way, n], z1_r.at[way, n], dev),
                remote(zs1.at[n, way], zs1r.at[n, way], t1_s.at[way, n], t1_r.at[way, n], dev))

    def second(n, way):
        dev = right if way == 0 else left
        src, dst = (zqa, zqar) if way == 0 else (zqb, zqbr)
        return (remote(src.at[n], dst.at[n], z2_s.at[way, n], z2_r.at[way, n], dev),
                remote(zs2.at[n, way], zs2r.at[n, way], t2_s.at[way, n], t2_r.at[way, n], dev))

    def peak(a):
        return jnp.maximum(jnp.max(jnp.max(jnp.abs(a), axis=0), axis=0, keepdims=True), TINY)

    def stage_a(n):
        take_halo(n + 1)
        diffuse(n)
        backward(n, 0, sib)
        share(n).start()
        backward(n, 1, own)

    def stage_b(n):
        share(n).wait_recv()
        for i in (0, 1, 3):
            own[n, i] = own[n, i] + sibr[n, i]
        far = own[n, 2] + sibr[n, 2]
        for way in range(2):
            if way == 0:
                a = jnp.concatenate([far[:HALF], own[n, 1, HALF:GLEV]], axis=0)
            else:
                a = jnp.concatenate([own[n, 3, 0:HALF], far[HALF:]], axis=0)
            top = peak(a)
            zs1[n, way] = top * (1.0 / 32767.0)
            zq1[n, way] = pack(a, top[None])
            each(first(n, way), "start")

    def stage_c(n):
        each(first(n, 0), "wait_recv")
        got = zq1r[n, 0].astype(F32) * zs1r[n, 0][None]
        a = own[n, 1, 0:HALF] + got[:HALF]
        top = peak(a)
        zs2[n, 0] = top * (1.0 / 32767.0)
        zqa[n] = pack(a, top[None])
        each(second(n, 0), "start")
        own[n, 0, HALF:GLEV] = own[n, 0, HALF:GLEV] + got[HALF:]
        each(first(n, 1), "wait_recv")
        got = zq1r[n, 1].astype(F32) * zs1r[n, 1][None]
        a = own[n, 3, HALF:GLEV] + got[HALF:]
        top = peak(a)
        zs2[n, 1] = top * (1.0 / 32767.0)
        zqb[n] = pack(a, top[None])
        each(second(n, 1), "start")
        own[n, 0, 0:HALF] = own[n, 0, 0:HALF] + got[:HALF]

    def stage_d(n):
        each(second(n, 0), "wait_recv")
        out_ref[0:HALF, chunk_rows(n), :] = own[n, 0, 0:HALF] + zqar[n].astype(F32) * zs2r[n, 0][None]
        each(second(n, 1), "wait_recv")
        out_ref[HALF:GLEV, chunk_rows(n), :] = own[n, 0, HALF:GLEV] + zqbr[n].astype(F32) * zs2r[n, 1][None]

    take_halo(0)

    def pipe(it, carry):
        pl.when(it < CHUNKS)(lambda: stage_a(it))
        pl.when(it > 0)(lambda: stage_b(it - 1))
        return carry

    def run(stage):
        def step(n, carry):
            stage(n)
            return carry
        lax.fori_loop(0, CHUNKS, step, 0)

    lax.fori_loop(0, CHUNKS + 1, pipe, 0)
    run(stage_c)
    run(stage_d)

    for j in range(1, GROUPS):
        send_modes(j).wait_send()

    @pl.when(has_next)
    def _():
        nu_up.wait_send()
        for i in range(MSGS):
            each(halo(i, 0), "wait_send")

    @pl.when(has_prev)
    def _():
        nu_down.wait_send()
        for i in range(MSGS):
            each(halo(i, 1), "wait_send")

    def sent(n):
        share(n).wait_send()
        for way in range(2):
            each(first(n, way), "wait_send")
            each(second(n, way), "wait_send")

    run(sent)


def tiles(a):
    lev = a.shape[0]
    return a.reshape(lev, ROWS, TILES, 128).transpose(0, 2, 1, 3).reshape(lev, TILES * ROWS, 128)


def untiles(a):
    lev = a.shape[0]
    return a.reshape(lev, TILES, ROWS, 128).transpose(0, 2, 1, 3).reshape(lev, ROWS, NLON)


def body(anomalies, vector, modes, order, weights, diffusivity):
    vmem, dma = pltpu.VMEM, pltpu.SemaphoreType.DMA
    hbm, smem = pl.BlockSpec(memory_space=pl.ANY), pl.BlockSpec(memory_space=pltpu.SMEM)
    rows = TILES * ROWS
    out = pl.pallas_call(
        kernel,
        out_shape=jax.ShapeDtypeStruct((GLEV, rows, 128), F32),
        in_specs=[hbm, hbm, hbm, smem, smem, hbm],
        out_specs=pl.BlockSpec(memory_space=pltpu.VMEM),
        scratch_shapes=[
            vmem((LEV, rows, 128), BF16),
            vmem((LEV, rows, 128), F32),
            vmem((2, LEV), F32),
            vmem((ROWS, NLON), F32),
            vmem((GROUPS, MODES, 256), F32),
            vmem((2, ROWS, NLON), F32),
            vmem((CHUNKS, LEV * 8, 256), BF16),
            vmem((CHUNKS, LEV * 8, 256), BF16),
            vmem((256, LEV * 8), BF16),
            vmem((2, 4 * LEV, 256), BF16),
            vmem((256, LEV * 8), BF16),
            vmem((2, 4 * LEV, 384), BF16),
            vmem((EXT, MODES, PADDED), F32),
            vmem((5, EXT - 2, 8, PADDED), F32),
            vmem((ROWS, MODES, WIDE), F32),
            vmem((384, 256), BF16),
            vmem((ROWS, MODES, PADDED), I16),
            vmem((1, PADDED), F32),
            vmem((2, ROWS, MODES, PADDED), I16),
            vmem((2, 1, PADDED), F32),
            vmem((CHUNKS, 4, GLEV, SUB, 128), F32),
            vmem((CHUNKS, 4, GLEV, SUB, 128), F32),
            vmem((CHUNKS, 4, GLEV, SUB, 128), F32),
            vmem((CHUNKS, 2, GLEV, SUB, 128), I16),
            vmem((CHUNKS, 2, 1, 128), F32),
            vmem((CHUNKS, 2, GLEV, SUB, 128), I16),
            vmem((CHUNKS, 2, 1, 128), F32),
            vmem((CHUNKS, HALF, SUB, 128), I16),
            vmem((CHUNKS, GLEV - HALF, SUB, 128), I16),
            vmem((CHUNKS, 2, 1, 128), F32),
            vmem((CHUNKS, HALF, SUB, 128), I16),
            vmem((CHUNKS, GLEV - HALF, SUB, 128), I16),
            vmem((CHUNKS, 2, 1, 128), F32),
            dma((2 + 2 * CHUNKS,)),
            dma((GROUPS,)), dma((GROUPS,)), dma((2,)), dma((2,)),
            dma((2, MSGS)), dma((2, MSGS)), dma((2, MSGS)), dma((2, MSGS)),
            dma((CHUNKS,)), dma((CHUNKS,)),
            dma((2, CHUNKS)), dma((2, CHUNKS)), dma((2, CHUNKS)), dma((2, CHUNKS)),
            dma((2, CHUNKS)), dma((2, CHUNKS)), dma((2, CHUNKS)), dma((2, CHUNKS)),
        ],
        compiler_params=pltpu.CompilerParams(
            collective_id=0, has_side_effects=True, vmem_limit_bytes=56 * 2**20),
    )(tiles(anomalies[0]), tiles(vector), modes, order, weights, diffusivity)
    return untiles(out)


def solution(mesh):
    return jax.shard_map(
        body,
        mesh=mesh,
        in_specs=(
            P("mode", None, "space", None),
            P(None, "space", None),
            P("mode", None),
            P(),
            P(),
            P("space", None),
        ),
        out_specs=P("mode", "space", None),
        check_vma=False,
    )
```

```python
import jax
import jax.numpy as jnp
from jax import lax
from jax.experimental import pallas as pl
from jax.experimental.pallas import tpu as pltpu
from jax.sharding import PartitionSpec as P

LEV, NLON, DIFF, MODES, ROWS = 136, 2048, 4, 16, 4
GROUPS = 8
GLEV = LEV // GROUPS
TILES = NLON // 128
CHUNKS = 4
SUB = TILES * ROWS // CHUNKS
WIDE = NLON // CHUNKS
PADDED = NLON + 256
EXT = ROWS + 2 * DIFF
HALF = (GLEV + 1) // 2
MSGS = CHUNKS + 1
TINY = 1e-33
F32, BF16, I16 = jnp.float32, jnp.bfloat16, jnp.int16


def split(a):
    hi = a.astype(BF16)
    return hi, (a - hi.astype(F32)).astype(BF16)


def pack(a, top):
    return jnp.round(a * (32767.0 / top)).astype(I16)


def kernel(x_hbm, v_hbm, modes_hbm, order_hbm, weights_hbm, diff_hbm, out_hbm,
           order_ref, weights_ref, xs, vs, mine, nu, mall, nuext, phi, plo, spread, pick, fwd, bwd, field, face, loc, lcat,
           hq, hsc, hqr, hscr, sib, sibr, own, zq1, zs1, zq1r, zs1r, zqa, zqb, zs2, zqar, zqbr, zs2r,
           lsem, osem, m_s, m_r, d_s, d_r, hq_s, hq_r, hs_s, hs_r, sb_s, sb_r,
           z1_s, z1_r, t1_s, t1_r, z2_s, z2_r, t2_s, t2_r):
    me = lax.axis_index("mode")
    place = lax.axis_index("space")
    ring, core = me // 2, me % 2
    has_prev = place > 0
    has_next = place < lax.axis_size("space") - 1
    right = {"mode": ((ring + 1) % 4) * 2 + core}
    left = {"mode": ((ring + 3) % 4) * 2 + core}
    partner = {"mode": ring * 2 + 1 - core}
    before, after = {"space": place - 1}, {"space": place + 1}

    def remote(src, dst, ss, rs, dev):
        return pltpu.make_async_remote_copy(
            src_ref=src, dst_ref=dst, send_sem=ss, recv_sem=rs, device_id=dev,
            device_id_type=pl.DeviceIdType.MESH)

    def chunk_rows(n):
        return pl.ds(pl.multiple_of(n * SUB, SUB), SUB)

    get_modes = pltpu.make_async_copy(modes_hbm, mine, lsem.at[0])
    get_nu = pltpu.make_async_copy(diff_hbm, nu, lsem.at[1])

    def get_x(n):
        return pltpu.make_async_copy(x_hbm.at[:, chunk_rows(n)], xs.at[:, chunk_rows(n)], lsem.at[2 + n])

    def get_v(n):
        return pltpu.make_async_copy(v_hbm.at[:, chunk_rows(n)], vs.at[:, chunk_rows(n)], lsem.at[2 + CHUNKS + n])

    get_order = pltpu.make_async_copy(order_hbm, order_ref, lsem.at[2 + 2 * CHUNKS])
    get_weights = pltpu.make_async_copy(weights_hbm, weights_ref, lsem.at[3 + 2 * CHUNKS])
    for copy in (get_modes, get_nu, get_order, get_weights):
        copy.start()
    for n in range(CHUNKS):
        get_x(n).start()
        get_v(n).start()

    barrier = pltpu.get_barrier_semaphore()

    def greet(dev):
        pl.semaphore_signal(barrier, inc=1, device_id=dev, device_id_type=pl.DeviceIdType.MESH)

    for j in range(1, GROUPS):
        greet({"mode": (me + j) % GROUPS})
    pl.when(has_prev)(lambda: greet(before))
    pl.when(has_next)(lambda: greet(after))

    lane_level = lax.broadcasted_iota(jnp.int32, (256, LEV * 8), 1) >> 3
    spread[...] = jnp.where(lane_level == lax.broadcasted_iota(jnp.int32, (256, LEV * 8), 0), 1.0, 0.0).astype(BF16)
    get_modes.wait()
    mall[0] = mine[...]
    get_nu.wait()
    get_order.wait()
    get_weights.wait()

    def products(n):
        get_x(n).wait()
        get_v(n).wait()

        for b in range(LEV // 8):
            lev = slice(b * 8, b * 8 + 8)
            p = xs[lev, chunk_rows(n), :].astype(F32) * vs[lev, chunk_rows(n), :]
            for h in range(2):
                hi, lo = split(p[:, 8 * h : 8 * h + 8, :].reshape(64, 128))
                phi[n, b * 64 : b * 64 + 64, 128 * h : 128 * h + 128] = hi
                plo[n, b * 64 : b * 64 + 64, 128 * h : 128 * h + 128] = lo

    pl.semaphore_wait(barrier, GROUPS - 1 + has_prev.astype(jnp.int32) + has_next.astype(jnp.int32))

    def send_modes(j):
        return remote(mall.at[0], mall.at[j], m_s.at[j], m_r.at[j], {"mode": (me + j) % GROUPS})

    for j in range(1, GROUPS):
        send_modes(j).start()
    nu_up = remote(nu, nuext.at[0], d_s.at[0], d_r.at[0], after)
    nu_down = remote(nu, nuext.at[1], d_s.at[1], d_r.at[1], before)
    pl.when(has_next)(lambda: nu_up.start())
    pl.when(has_prev)(lambda: nu_down.start())

    def run(stage):
        def step(n, carry):
            stage(n)
            return carry
        lax.fori_loop(0, CHUNKS, step, 0)

    for i in range(GROUPS):
        c = 1 - core if i < 4 else core
        group = ((ring + i) % 4) * 2 + c
        level = group * GLEV + (lax.broadcasted_iota(jnp.int32, (LEV, 256), 0) >> 3)
        pick[i // 4, (i % 4) * LEV : (i % 4 + 1) * LEV, :] = jnp.where(
            lax.broadcasted_iota(jnp.int32, (LEV, 256), 1) == level, 1.0, 0.0).astype(BF16)

    run(products)

    for j in range(1, GROUPS):
        send_modes(j).wait_recv()
    modes = jnp.zeros((MODES, LEV), F32)
    for j in range(GROUPS):
        row = lax.broadcasted_iota(jnp.int32, (MODES, LEV), 0) - 2 * ((me - j + GROUPS) % GROUPS)
        modes = jnp.where(row == 0, mall[j, 0:1, :], jnp.where(row == 1, mall[j, 1:2, :], modes))
    modes = jnp.concatenate([modes, jnp.zeros((MODES, 256 - LEV), F32)], axis=1)
    modes_hi, modes_lo = split(modes)

    both = jnp.dot(jnp.concatenate([modes_hi, modes_lo], axis=0), spread[...], preferred_element_type=F32)
    sub = lax.broadcasted_iota(jnp.int32, (MODES, LEV * 8), 1) & 7
    for half in range(2):
        rows = both[half * MODES : (half + 1) * MODES]
        for q in range(8):
            fwd[half * 128 + q * MODES : half * 128 + (q + 1) * MODES, :] = jnp.where(sub == q, rows, 0.0).astype(BF16)

    def peak(a):
        return jnp.maximum(jnp.max(jnp.max(jnp.abs(a), axis=0), axis=0, keepdims=True), TINY)

    def project(n):
        main = jnp.dot(fwd[...], phi[n], preferred_element_type=F32)
        rest = jnp.dot(fwd[0:128, :], plo[n], preferred_element_type=F32)
        total = main[0:128] + main[128:256] + rest
        for par in range(2):
            for r in range(ROWS):
                for h in range(2):
                    at = (1 + 4 * n + 2 * h + par) * 128
                    q = (par * ROWS + r) * MODES
                    field[DIFF + r, :, at : at + 128] = total[q : q + MODES, h * 128 : h * 128 + 128]

    def halo_lanes(i):
        if isinstance(i, int) and i == 0:
            return pl.ds(0, 256)
        return pl.ds(pl.multiple_of(i * WIDE - WIDE + 256, 128), WIDE)

    def halo(i, way):
        lanes = halo_lanes(i)
        dev = after if way == 0 else before
        return (remote(hq.at[:, :, lanes], hqr.at[way, :, :, lanes], hq_s.at[way, i], hq_r.at[way, i], dev),
                remote(hsc.at[:, lanes], hscr.at[way, :, lanes], hs_s.at[way, i], hs_r.at[way, i], dev))

    def each(copies, what):
        for copy in copies:
            getattr(copy, what)()

    def send_halo(i):
        lanes = halo_lanes(i)
        u = field[DIFF : DIFF + ROWS, :, lanes]
        top = peak(u)
        hsc[:, lanes] = top * (1.0 / 32767.0)
        hq[:, :, lanes] = pack(u, top[None])
        pl.when(has_next)(lambda: each(halo(i, 0), "start"))
        pl.when(has_prev)(lambda: each(halo(i, 1), "start"))

    own_rows = slice(DIFF, DIFF + ROWS)
    project(3)
    field[own_rows, :, 0:128] = field[own_rows, :, NLON : NLON + 128]
    project(0)
    field[own_rows, :, NLON + 128 : PADDED] = field[own_rows, :, 128:256]
    send_halo(0)
    project(1)
    send_halo(1)
    project(2)
    for i in range(2, MSGS):
        send_halo(i)

    rep_hi = jnp.concatenate([modes_hi] * 8, axis=0)
    rep_lo = jnp.concatenate([modes_lo] * 8, axis=0)
    same = (lax.broadcasted_iota(jnp.int32, (4 * LEV, 128), 0) & 7) == (lax.broadcasted_iota(jnp.int32, (4 * LEV, 128), 1) >> 4)
    last = (((1,), (1,)), ((), ()))
    for part in range(2):
        hi = lax.dot_general(pick[part], rep_hi, last, preferred_element_type=F32)
        lo = lax.dot_general(pick[part], rep_lo, last, preferred_element_type=F32)
        hi = jnp.where(same, hi, 0.0).astype(BF16)
        bwd[part, :, 0:128] = hi
        bwd[part, :, 128:256] = hi
        bwd[part, :, 256:384] = jnp.where(same, lo, 0.0).astype(BF16)

    @pl.when(has_prev)
    def _():
        nu_up.wait_recv()

    @pl.when(has_next)
    def _():
        nu_down.wait_recv()

    @pl.when(jnp.logical_not(has_prev))
    def _():
        nuext[0] = jnp.zeros((ROWS, NLON), F32)
        field[0:DIFF] = jnp.zeros((DIFF, MODES, PADDED), F32)

    @pl.when(jnp.logical_not(has_next))
    def _():
        nuext[1] = jnp.zeros((ROWS, NLON), F32)
        field[DIFF + ROWS : EXT] = jnp.zeros((DIFF, MODES, PADDED), F32)

    def nu_row(a):
        src = nuext[0] if a < DIFF else nu[...] if a < DIFF + ROWS else nuext[1]
        r = a % ROWS
        return jnp.broadcast_to(src[r : r + 1, :], (8, NLON))

    for a in range(EXT - 1):
        here = nu_row(a)
        for c, other in enumerate((pltpu.roll(here, NLON - 1, 1), nu_row(a + 1))):
            arm = 0.5 * (here + other)
            face[c, a, :, 128 : NLON + 128] = arm
            face[c, a, :, 0:128] = arm[:, NLON - 128 : NLON]
            face[c, a, :, NLON + 128 : PADDED] = arm[:, 0:128]

    weight = jnp.float32(0.0)
    for s in range(GROUPS):
        weight = weight + jnp.where(order_ref[s] == me, weights_ref[s], 0.0)

    def take_halo(i):
        lanes = halo_lanes(i)

        @pl.when(has_prev)
        def _():
            each(halo(i, 0), "wait_recv")
            field[0:DIFF, :, lanes] = hqr[0, :, :, lanes].astype(F32) * hscr[0, :, lanes][None]

        @pl.when(has_next)
        def _():
            each(halo(i, 1), "wait_recv")
            field[DIFF + ROWS : EXT, :, lanes] = hqr[1, :, :, lanes].astype(F32) * hscr[1, :, lanes][None]

    window = WIDE + 256
    top_mask, low_mask = has_prev.astype(F32), has_next.astype(F32)

    def diffuse(n):
        lanes = pl.ds(pl.multiple_of(n * WIDE, 128), window)
        def both_halves(c, a):
            arm = face[c, a, :, lanes]
            return jnp.concatenate([arm, arm], axis=0)

        u = [field[a, :, lanes] for a in range(EXT)]
        for s in range(1, DIFF + 1):
            new = []
            north = both_halves(1, s - 1) * (u[1] - u[0])
            for a in range(s, EXT - s):
                c, down = u[a - s + 1], u[a - s + 2]
                south = both_halves(1, a) * (down - c)
                east = both_halves(0, a) * (pltpu.roll(c, window - 1, 1) - c)
                total = c + (south - north) + (east - pltpu.roll(east, 1, 1))
                if a < DIFF:
                    total = total * top_mask
                elif a >= DIFF + ROWS:
                    total = total * low_mask
                new.append(total)
                north = south
            u = new
        for r in range(ROWS):
            loc[r] = weight * u[r][:, 128 : 128 + WIDE]
        for par in range(2):
            for r in range(ROWS):
                q = (par * ROWS + r) * MODES
                for h in range(2):
                    t = (2 * h + par) * 128
                    hi, lo = split(loc[r, :, t : t + 128])
                    cols = slice(h * 128, h * 128 + 128)
                    lcat[q : q + MODES, cols] = hi
                    lcat[128 + q : 128 + q + MODES, cols] = lo
                    lcat[256 + q : 256 + q + MODES, cols] = hi

    def share(n, i):
        return remote(sib.at[n, i], sibr.at[n, i], sb_s.at[n, i], sb_r.at[n, i], partner)

    def backward(n, part, dst):
        back = jnp.dot(bwd[part], lcat[...], preferred_element_type=F32)
        c = core if part else 1 - core
        for i in (2, 1, 3, 0):
            group = ((ring + i) % 4) * 2 + c
            xg = xs[pl.ds(group * GLEV, GLEV), chunk_rows(n), :].astype(F32)
            for h in range(2):
                b = back[i * LEV : (i + 1) * LEV, h * 128 : h * 128 + 128].reshape(GLEV, 8, 128)
                dst[n, i, :, 8 * h : 8 * h + 8, :] = xg[:, 8 * h : 8 * h + 8, :] * b
            if part == 0:
                share(n, i).start()

    def first(n, way):
        dev = right if way == 0 else left
        return (remote(zq1.at[n, way], zq1r.at[n, way], z1_s.at[way, n], z1_r.at[way, n], dev),
                remote(zs1.at[n, way], zs1r.at[n, way], t1_s.at[way, n], t1_r.at[way, n], dev))

    def second(n, way):
        dev = right if way == 0 else left
        src, dst = (zqa, zqar) if way == 0 else (zqb, zqbr)
        return (remote(src.at[n], dst.at[n], z2_s.at[way, n], z2_r.at[way, n], dev),
                remote(zs2.at[n, way], zs2r.at[n, way], t2_s.at[way, n], t2_r.at[way, n], dev))

    def stage_a(n):
        take_halo(n + 1)
        diffuse(n)
        backward(n, 0, sib)
        backward(n, 1, own)

    def stage_b(n):
        share(n, 2).wait_recv()
        far = own[n, 2] + sibr[n, 2]
        for way in range(2):
            i = 1 if way == 0 else 3
            share(n, i).wait_recv()
            own[n, i] = own[n, i] + sibr[n, i]
            if way == 0:
                a = jnp.concatenate([far[:HALF], own[n, 1, HALF:GLEV]], axis=0)
            else:
                a = jnp.concatenate([own[n, 3, 0:HALF], far[HALF:]], axis=0)
            top = peak(a)
            zs1[n, way] = top * (1.0 / 32767.0)
            zq1[n, way] = pack(a, top[None])
            each(first(n, way), "start")
        share(n, 0).wait_recv()
        own[n, 0] = own[n, 0] + sibr[n, 0]

    def stage_c(n):
        each(first(n, 0), "wait_recv")
        got = zq1r[n, 0].astype(F32) * zs1r[n, 0][None]
        a = own[n, 1, 0:HALF] + got[:HALF]
        top = peak(a)
        zs2[n, 0] = top * (1.0 / 32767.0)
        zqa[n] = pack(a, top[None])
        each(second(n, 0), "start")
        own[n, 0, HALF:GLEV] = own[n, 0, HALF:GLEV] + got[HALF:]
        each(first(n, 1), "wait_recv")
        got = zq1r[n, 1].astype(F32) * zs1r[n, 1][None]
        a = own[n, 3, HALF:GLEV] + got[HALF:]
        top = peak(a)
        zs2[n, 1] = top * (1.0 / 32767.0)
        zqb[n] = pack(a, top[None])
        each(second(n, 1), "start")
        own[n, 0, 0:HALF] = own[n, 0, 0:HALF] + got[:HALF]

    def stage_d(n):
        each(second(n, 0), "wait_recv")
        own[n, 0, 0:HALF] = own[n, 0, 0:HALF] + zqar[n].astype(F32) * zs2r[n, 0][None]
        each(second(n, 1), "wait_recv")
        own[n, 0, HALF:GLEV] = own[n, 0, HALF:GLEV] + zqbr[n].astype(F32) * zs2r[n, 1][None]

        put(n).start()

    def put(n):
        return pltpu.make_async_copy(own.at[n, 0], out_hbm.at[:, chunk_rows(n)], osem.at[n])

    take_halo(0)

    def pipe(it, carry):
        pl.when(it < CHUNKS)(lambda: stage_a(it))
        pl.when(it != 1)(lambda: stage_b(jnp.maximum(it - 1, 0)))
        return carry

    lax.fori_loop(0, CHUNKS + 1, pipe, 0)
    run(stage_c)
    run(stage_d)

    for j in range(1, GROUPS):
        send_modes(j).wait_send()

    @pl.when(has_next)
    def _():
        nu_up.wait_send()
        for i in range(MSGS):
            each(halo(i, 0), "wait_send")

    @pl.when(has_prev)
    def _():
        nu_down.wait_send()
        for i in range(MSGS):
            each(halo(i, 1), "wait_send")

    def sent(n):
        for i in range(4):
            share(n, i).wait_send()
        put(n).wait()
        for way in range(2):
            each(first(n, way), "wait_send")
            each(second(n, way), "wait_send")

    run(sent)


def tiles(a):
    lev = a.shape[0]
    return a.reshape(lev, ROWS, TILES, 128).transpose(0, 2, 1, 3).reshape(lev, TILES * ROWS, 128)


def untiles(a):
    lev = a.shape[0]
    return a.reshape(lev, TILES, ROWS, 128).transpose(0, 2, 1, 3).reshape(lev, ROWS, NLON)


def body(anomalies, vector, modes, order, weights, diffusivity):
    vmem, dma = pltpu.VMEM, pltpu.SemaphoreType.DMA
    hbm = pl.BlockSpec(memory_space=pltpu.HBM)
    rows = TILES * ROWS
    out = pl.pallas_call(
        kernel,
        out_shape=jax.ShapeDtypeStruct((GLEV, rows, 128), F32),
        in_specs=[hbm] * 6,
        out_specs=pl.BlockSpec(memory_space=pl.ANY),
        scratch_shapes=[
            pltpu.SMEM((GROUPS,), jnp.int32),
            pltpu.SMEM((GROUPS,), F32),
            vmem((LEV, rows, 128), BF16),
            vmem((LEV, rows, 128), F32),
            vmem((2, LEV), F32),
            vmem((ROWS, NLON), F32),
            vmem((GROUPS, 2, LEV), F32),
            vmem((2, ROWS, NLON), F32),
            vmem((CHUNKS, LEV * 8, 256), BF16),
            vmem((CHUNKS, LEV * 8, 256), BF16),
            vmem((256, LEV * 8), BF16),
            vmem((2, 4 * LEV, 256), BF16),
            vmem((256, LEV * 8), BF16),
            vmem((2, 4 * LEV, 384), BF16),
            vmem((EXT, MODES, PADDED), F32),
            vmem((2, EXT - 1, 8, PADDED), F32),
            vmem((ROWS, MODES, WIDE), F32),
            vmem((384, 256), BF16),
            vmem((ROWS, MODES, PADDED), I16),
            vmem((1, PADDED), F32),
            vmem((2, ROWS, MODES, PADDED), I16),
            vmem((2, 1, PADDED), F32),
            vmem((CHUNKS, 4, GLEV, SUB, 128), F32),
            vmem((CHUNKS, 4, GLEV, SUB, 128), F32),
            vmem((CHUNKS, 4, GLEV, SUB, 128), F32),
            vmem((CHUNKS, 2, GLEV, SUB, 128), I16),
            vmem((CHUNKS, 2, 1, 128), F32),
            vmem((CHUNKS, 2, GLEV, SUB, 128), I16),
            vmem((CHUNKS, 2, 1, 128), F32),
            vmem((CHUNKS, HALF, SUB, 128), I16),
            vmem((CHUNKS, GLEV - HALF, SUB, 128), I16),
            vmem((CHUNKS, 2, 1, 128), F32),
            vmem((CHUNKS, HALF, SUB, 128), I16),
            vmem((CHUNKS, GLEV - HALF, SUB, 128), I16),
            vmem((CHUNKS, 2, 1, 128), F32),
            dma((4 + 2 * CHUNKS,)), dma((CHUNKS,)),
            dma((GROUPS,)), dma((GROUPS,)), dma((2,)), dma((2,)),
            dma((2, MSGS)), dma((2, MSGS)), dma((2, MSGS)), dma((2, MSGS)),
            dma((CHUNKS, 4)), dma((CHUNKS, 4)),
            dma((2, CHUNKS)), dma((2, CHUNKS)), dma((2, CHUNKS)), dma((2, CHUNKS)),
            dma((2, CHUNKS)), dma((2, CHUNKS)), dma((2, CHUNKS)), dma((2, CHUNKS)),
        ],
        compiler_params=pltpu.CompilerParams(
            collective_id=0, has_side_effects=True, vmem_limit_bytes=53 * 2**20),
    )(*[pltpu.with_memory_space_constraint(a, pltpu.HBM) for a in (tiles(anomalies[0]), tiles(vector), modes, order, weights, diffusivity)])
    return untiles(out)


def solution(mesh):
    return jax.shard_map(
        body,
        mesh=mesh,
        in_specs=(
            P("mode", None, "space", None),
            P(None, "space", None),
            P("mode", None),
            P(),
            P(),
            P("space", None),
        ),
        out_specs=P("mode", "space", None),
        check_vma=False,
    )
```

```python
import jax
import jax.numpy as jnp
from jax import lax
from jax.experimental import pallas as pl
from jax.experimental.pallas import tpu as pltpu
from jax.sharding import PartitionSpec as P

LEV, NLON, DIFF, MODES, ROWS = 136, 2048, 4, 16, 4
GROUPS = 8
GLEV = LEV // GROUPS
TILES = NLON // 128
CHUNKS = 4
SUB = TILES * ROWS // CHUNKS
WIDE = NLON // CHUNKS
PADDED = NLON + 256
EXT = ROWS + 2 * DIFF
HALF = (GLEV + 1) // 2
MSGS = CHUNKS + 1
TINY = 1e-33
F32, BF16, I16 = jnp.float32, jnp.bfloat16, jnp.int16


def split(a):
    hi = a.astype(BF16)
    return hi, (a - hi.astype(F32)).astype(BF16)


def pack(a, top):
    return jnp.round(a * (32767.0 / top)).astype(I16)


def kernel(x_hbm, v_hbm, modes_hbm, order_hbm, weights_hbm, diff_hbm, out_hbm,
           order_ref, weights_ref, xs, vs, mine, nu, mall, nuext, phi, plo, spread, pick, fwd, bwd, field, face, loc, lcat,
           hq, hsc, hqr, hscr, xsib, lsib, own, zq1, zs1, zq1r, zs1r, zqa, zqb, zs2, zqar, zqbr, zs2r,
           lsem, osem, m_s, m_r, d_s, d_r, hq_s, hq_r, hs_s, hs_r, sb_s, sb_r, xb_s, xb_r,
           z1_s, z1_r, t1_s, t1_r, z2_s, z2_r, t2_s, t2_r):
    me = lax.axis_index("mode")
    place = lax.axis_index("space")
    ring, core = me // 2, me % 2
    has_prev = place > 0
    has_next = place < lax.axis_size("space") - 1
    right = {"mode": ((ring + 1) % 4) * 2 + core}
    left = {"mode": ((ring + 3) % 4) * 2 + core}
    partner = {"mode": ring * 2 + 1 - core}
    before, after = {"space": place - 1}, {"space": place + 1}

    def remote(src, dst, ss, rs, dev):
        return pltpu.make_async_remote_copy(
            src_ref=src, dst_ref=dst, send_sem=ss, recv_sem=rs, device_id=dev,
            device_id_type=pl.DeviceIdType.MESH)

    def chunk_rows(n):
        return pl.ds(pl.multiple_of(n * SUB, SUB), SUB)

    get_modes = pltpu.make_async_copy(modes_hbm, mine, lsem.at[0])
    get_nu = pltpu.make_async_copy(diff_hbm, nu, lsem.at[1])

    def get_x(n):
        return pltpu.make_async_copy(x_hbm.at[:, chunk_rows(n)], xs.at[:, chunk_rows(n)], lsem.at[2 + n])

    def get_v(n):
        return pltpu.make_async_copy(v_hbm.at[:, chunk_rows(n)], vs.at[:, chunk_rows(n)], lsem.at[2 + CHUNKS + n])

    get_order = pltpu.make_async_copy(order_hbm, order_ref, lsem.at[2 + 2 * CHUNKS])
    get_weights = pltpu.make_async_copy(weights_hbm, weights_ref, lsem.at[3 + 2 * CHUNKS])
    for copy in (get_modes, get_nu, get_order, get_weights):
        copy.start()
    for n in range(CHUNKS):
        get_x(n).start()
        get_v(n).start()

    barrier = pltpu.get_barrier_semaphore()

    def greet(dev):
        pl.semaphore_signal(barrier, inc=1, device_id=dev, device_id_type=pl.DeviceIdType.MESH)

    for j in range(1, GROUPS):
        greet({"mode": (me + j) % GROUPS})
    pl.when(has_prev)(lambda: greet(before))
    pl.when(has_next)(lambda: greet(after))

    lane_level = lax.broadcasted_iota(jnp.int32, (256, LEV * 8), 1) >> 3
    spread[...] = jnp.where(lane_level == lax.broadcasted_iota(jnp.int32, (256, LEV * 8), 0), 1.0, 0.0).astype(BF16)
    get_modes.wait()
    mall[0] = mine[...]
    get_nu.wait()
    get_order.wait()
    get_weights.wait()

    def products(n):
        get_x(n).wait()
        get_v(n).wait()

        for b in range(LEV // 8):
            lev = slice(b * 8, b * 8 + 8)
            p = xs[lev, chunk_rows(n), :].astype(F32) * vs[lev, chunk_rows(n), :]
            for h in range(2):
                hi, lo = split(p[:, 8 * h : 8 * h + 8, :].reshape(64, 128))
                phi[n, b * 64 : b * 64 + 64, 128 * h : 128 * h + 128] = hi
                plo[n, b * 64 : b * 64 + 64, 128 * h : 128 * h + 128] = lo

    pl.semaphore_wait(barrier, GROUPS - 1 + has_prev.astype(jnp.int32) + has_next.astype(jnp.int32))

    def send_modes(j):
        return remote(mall.at[0], mall.at[j], m_s.at[j], m_r.at[j], {"mode": (me + j) % GROUPS})

    for j in range(1, GROUPS):
        send_modes(j).start()
    nu_up = remote(nu, nuext.at[0], d_s.at[0], d_r.at[0], after)
    nu_down = remote(nu, nuext.at[1], d_s.at[1], d_r.at[1], before)
    pl.when(has_next)(lambda: nu_up.start())
    pl.when(has_prev)(lambda: nu_down.start())

    def run(stage):
        def step(n, carry):
            stage(n)
            return carry
        lax.fori_loop(0, CHUNKS, step, 0)

    def levels_of(i, c):
        return pl.ds((((ring + i) % 4) * 2 + c) * GLEV, GLEV)

    for i in range(4):
        level = (((ring + i) % 4) * 2 + core) * GLEV + (lax.broadcasted_iota(jnp.int32, (LEV, 256), 0) >> 3)
        pick[i * LEV : (i + 1) * LEV, :] = jnp.where(
            lax.broadcasted_iota(jnp.int32, (LEV, 256), 1) == level, 1.0, 0.0).astype(BF16)

    run(products)

    def lend(i):
        return remote(xs.at[levels_of(i, 1 - core)], xsib.at[i], xb_s.at[i], xb_r.at[i], partner)

    for i in range(4):
        lend(i).start()

    for j in range(1, GROUPS):
        send_modes(j).wait_recv()
    modes = jnp.zeros((MODES, LEV), F32)
    for j in range(GROUPS):
        row = lax.broadcasted_iota(jnp.int32, (MODES, LEV), 0) - 2 * ((me - j + GROUPS) % GROUPS)
        modes = jnp.where(row == 0, mall[j, 0:1, :], jnp.where(row == 1, mall[j, 1:2, :], modes))
    modes = jnp.concatenate([modes, jnp.zeros((MODES, 256 - LEV), F32)], axis=1)
    modes_hi, modes_lo = split(modes)

    both = jnp.dot(jnp.concatenate([modes_hi, modes_lo], axis=0), spread[...], preferred_element_type=F32)
    sub = lax.broadcasted_iota(jnp.int32, (MODES, LEV * 8), 1) & 7
    for half in range(2):
        rows = both[half * MODES : (half + 1) * MODES]
        for q in range(8):
            fwd[half * 128 + q * MODES : half * 128 + (q + 1) * MODES, :] = jnp.where(sub == q, rows, 0.0).astype(BF16)

    def peak(a):
        return jnp.maximum(jnp.max(jnp.max(jnp.abs(a), axis=0), axis=0, keepdims=True), TINY)

    def project(n):
        main = jnp.dot(fwd[...], phi[n], preferred_element_type=F32)
        rest = jnp.dot(fwd[0:128, :], plo[n], preferred_element_type=F32)
        total = main[0:128] + main[128:256] + rest
        for par in range(2):
            for r in range(ROWS):
                for h in range(2):
                    at = (1 + 4 * n + 2 * h + par) * 128
                    q = (par * ROWS + r) * MODES
                    field[DIFF + r, :, at : at + 128] = total[q : q + MODES, h * 128 : h * 128 + 128]

    def halo_lanes(i):
        if isinstance(i, int) and i == 0:
            return pl.ds(0, 256)
        return pl.ds(pl.multiple_of(i * WIDE - WIDE + 256, 128), WIDE)

    def halo(i, way):
        lanes = halo_lanes(i)
        dev = after if way == 0 else before
        return (remote(hq.at[:, :, lanes], hqr.at[way, :, :, lanes], hq_s.at[way, i], hq_r.at[way, i], dev),
                remote(hsc.at[:, lanes], hscr.at[way, :, lanes], hs_s.at[way, i], hs_r.at[way, i], dev))

    def each(copies, what):
        for copy in copies:
            getattr(copy, what)()

    def send_halo(i):
        lanes = halo_lanes(i)
        u = field[DIFF : DIFF + ROWS, :, lanes]
        top = peak(u)
        hsc[:, lanes] = top * (1.0 / 32767.0)
        hq[:, :, lanes] = pack(u, top[None])
        pl.when(has_next)(lambda: each(halo(i, 0), "start"))
        pl.when(has_prev)(lambda: each(halo(i, 1), "start"))

    own_rows = slice(DIFF, DIFF + ROWS)
    project(3)
    field[own_rows, :, 0:128] = field[own_rows, :, NLON : NLON + 128]
    project(0)
    field[own_rows, :, NLON + 128 : PADDED] = field[own_rows, :, 128:256]
    send_halo(0)
    project(1)
    send_halo(1)
    project(2)
    for i in range(2, MSGS):
        send_halo(i)

    rep_hi = jnp.concatenate([modes_hi] * 8, axis=0)
    rep_lo = jnp.concatenate([modes_lo] * 8, axis=0)
    same = (lax.broadcasted_iota(jnp.int32, (4 * LEV, 128), 0) & 7) == (lax.broadcasted_iota(jnp.int32, (4 * LEV, 128), 1) >> 4)
    last = (((1,), (1,)), ((), ()))
    hi = jnp.where(same, lax.dot_general(pick[...], rep_hi, last, preferred_element_type=F32), 0.0).astype(BF16)
    bwd[:, 0:128] = hi
    bwd[:, 128:256] = hi
    lo = lax.dot_general(pick[...], rep_lo, last, preferred_element_type=F32)
    bwd[:, 256:384] = jnp.where(same, lo, 0.0).astype(BF16)

    @pl.when(has_prev)
    def _():
        nu_up.wait_recv()

    @pl.when(has_next)
    def _():
        nu_down.wait_recv()

    @pl.when(jnp.logical_not(has_prev))
    def _():
        nuext[0] = jnp.zeros((ROWS, NLON), F32)
        field[0:DIFF] = jnp.zeros((DIFF, MODES, PADDED), F32)

    @pl.when(jnp.logical_not(has_next))
    def _():
        nuext[1] = jnp.zeros((ROWS, NLON), F32)
        field[DIFF + ROWS : EXT] = jnp.zeros((DIFF, MODES, PADDED), F32)

    def nu_row(a):
        src = nuext[0] if a < DIFF else nu[...] if a < DIFF + ROWS else nuext[1]
        r = a % ROWS
        return jnp.broadcast_to(src[r : r + 1, :], (8, NLON))

    for a in range(EXT - 1):
        here = nu_row(a)
        for c, other in enumerate((pltpu.roll(here, NLON - 1, 1), nu_row(a + 1))):
            arm = 0.5 * (here + other)
            face[c, a, :, 128 : NLON + 128] = arm
            face[c, a, :, 0:128] = arm[:, NLON - 128 : NLON]
            face[c, a, :, NLON + 128 : PADDED] = arm[:, 0:128]

    weight = jnp.float32(0.0)
    for s in range(GROUPS):
        weight = weight + jnp.where(order_ref[s] == me, weights_ref[s], 0.0)

    def take_halo(i):
        lanes = halo_lanes(i)

        @pl.when(has_prev)
        def _():
            each(halo(i, 0), "wait_recv")
            field[0:DIFF, :, lanes] = hqr[0, :, :, lanes].astype(F32) * hscr[0, :, lanes][None]

        @pl.when(has_next)
        def _():
            each(halo(i, 1), "wait_recv")
            field[DIFF + ROWS : EXT, :, lanes] = hqr[1, :, :, lanes].astype(F32) * hscr[1, :, lanes][None]

    window = WIDE + 256
    top_mask, low_mask = has_prev.astype(F32), has_next.astype(F32)

    def diffuse(n):
        lanes = pl.ds(pl.multiple_of(n * WIDE, 128), window)
        def both_halves(c, a):
            arm = face[c, a, :, lanes]
            return jnp.concatenate([arm, arm], axis=0)

        u = [field[a, :, lanes] for a in range(EXT)]
        for s in range(1, DIFF + 1):
            new = []
            north = both_halves(1, s - 1) * (u[1] - u[0])
            for a in range(s, EXT - s):
                c, down = u[a - s + 1], u[a - s + 2]
                south = both_halves(1, a) * (down - c)
                east = both_halves(0, a) * (pltpu.roll(c, window - 1, 1) - c)
                total = c + (south - north) + (east - pltpu.roll(east, 1, 1))
                if a < DIFF:
                    total = total * top_mask
                elif a >= DIFF + ROWS:
                    total = total * low_mask
                new.append(total)
                north = south
            u = new
        for r in range(ROWS):
            loc[r] = weight * u[r][:, 128 : 128 + WIDE]
        for par in range(2):
            for r in range(ROWS):
                q = (par * ROWS + r) * MODES
                for h in range(2):
                    t = (2 * h + par) * 128
                    hi, lo = split(loc[r, :, t : t + 128])
                    cols = slice(h * 128, h * 128 + 128)
                    lcat[n, q : q + MODES, cols] = hi
                    lcat[n, 128 + q : 128 + q + MODES, cols] = lo

    def share(n):
        return remote(lcat.at[n], lsib.at[n], sb_s.at[n], sb_r.at[n], partner)

    def backward(terms):
        return (jnp.dot(bwd[:, 0:256], terms[...], preferred_element_type=F32)
                + jnp.dot(bwd[:, 256:384], terms[0:128, :], preferred_element_type=F32))

    def times(back, i, x):
        return jnp.concatenate(
            [x[:, 8 * h : 8 * h + 8, :] * back[i * LEV : (i + 1) * LEV, h * 128 : h * 128 + 128].reshape(GLEV, 8, 128)
             for h in range(2)], axis=1)

    def first(n, way):
        dev = right if way == 0 else left
        return (remote(zq1.at[n, way], zq1r.at[n, way], z1_s.at[way, n], z1_r.at[way, n], dev),
                remote(zs1.at[n, way], zs1r.at[n, way], t1_s.at[way, n], t1_r.at[way, n], dev))

    def second(n, way):
        dev = right if way == 0 else left
        src, dst = (zqa, zqar) if way == 0 else (zqb, zqbr)
        return (remote(src.at[n], dst.at[n], z2_s.at[way, n], z2_r.at[way, n], dev),
                remote(zs2.at[n, way], zs2r.at[n, way], t2_s.at[way, n], t2_r.at[way, n], dev))

    def stage_a(n):
        take_halo(n + 1)
        diffuse(n)
        share(n).start()
        back = backward(lcat.at[n])
        for i in range(4):
            own[n, i] = times(back, i, xs[levels_of(i, core), chunk_rows(n), :].astype(F32))

    def stage_b(n):
        share(n).wait_recv()
        back = backward(lsib.at[n])

        def both(i):
            return own[n, i] + times(back, i, xsib[i, :, chunk_rows(n), :].astype(F32))

        far = both(2)
        for way in range(2):
            i = 1 if way == 0 else 3
            near = both(i)
            own[n, i] = near
            if way == 0:
                a = jnp.concatenate([far[:HALF], near[HALF:GLEV]], axis=0)
            else:
                a = jnp.concatenate([near[0:HALF], far[HALF:]], axis=0)
            top = peak(a)
            zs1[n, way] = top * (1.0 / 32767.0)
            zq1[n, way] = pack(a, top[None])
            each(first(n, way), "start")
        own[n, 0] = both(0)

    def stage_c(n):
        each(first(n, 0), "wait_recv")
        got = zq1r[n, 0].astype(F32) * zs1r[n, 0][None]
        a = own[n, 1, 0:HALF] + got[:HALF]
        top = peak(a)
        zs2[n, 0] = top * (1.0 / 32767.0)
        zqa[n] = pack(a, top[None])
        each(second(n, 0), "start")
        own[n, 0, HALF:GLEV] = own[n, 0, HALF:GLEV] + got[HALF:]
        each(first(n, 1), "wait_recv")
        got = zq1r[n, 1].astype(F32) * zs1r[n, 1][None]
        a = own[n, 3, HALF:GLEV] + got[HALF:]
        top = peak(a)
        zs2[n, 1] = top * (1.0 / 32767.0)
        zqb[n] = pack(a, top[None])
        each(second(n, 1), "start")
        own[n, 0, 0:HALF] = own[n, 0, 0:HALF] + got[:HALF]

    def stage_d(n):
        each(second(n, 0), "wait_recv")
        own[n, 0, 0:HALF] = own[n, 0, 0:HALF] + zqar[n].astype(F32) * zs2r[n, 0][None]
        each(second(n, 1), "wait_recv")
        own[n, 0, HALF:GLEV] = own[n, 0, HALF:GLEV] + zqbr[n].astype(F32) * zs2r[n, 1][None]

        put(n).start()

    def put(n):
        return pltpu.make_async_copy(own.at[n, 0], out_hbm.at[:, chunk_rows(n)], osem.at[n])

    take_halo(0)
    for i in range(4):
        lend(i).wait_recv()

    def pipe(it, carry):
        pl.when(it < CHUNKS)(lambda: stage_a(it))
        pl.when(it != 1)(lambda: stage_b(jnp.maximum(it - 1, 0)))
        return carry

    lax.fori_loop(0, CHUNKS + 1, pipe, 0)
    run(stage_c)
    run(stage_d)

    for j in range(1, GROUPS):
        send_modes(j).wait_send()
    for i in range(4):
        lend(i).wait_send()

    @pl.when(has_next)
    def _():
        nu_up.wait_send()
        for i in range(MSGS):
            each(halo(i, 0), "wait_send")

    @pl.when(has_prev)
    def _():
        nu_down.wait_send()
        for i in range(MSGS):
            each(halo(i, 1), "wait_send")

    def sent(n):
        share(n).wait_send()
        put(n).wait()
        for way in range(2):
            each(first(n, way), "wait_send")
            each(second(n, way), "wait_send")

    run(sent)


def tiles(a):
    lev = a.shape[0]
    return a.reshape(lev, ROWS, TILES, 128).transpose(0, 2, 1, 3).reshape(lev, TILES * ROWS, 128)


def untiles(a):
    lev = a.shape[0]
    return a.reshape(lev, TILES, ROWS, 128).transpose(0, 2, 1, 3).reshape(lev, ROWS, NLON)


def body(anomalies, vector, modes, order, weights, diffusivity):
    vmem, dma = pltpu.VMEM, pltpu.SemaphoreType.DMA
    hbm = pl.BlockSpec(memory_space=pltpu.HBM)
    rows = TILES * ROWS
    out = pl.pallas_call(
        kernel,
        out_shape=jax.ShapeDtypeStruct((GLEV, rows, 128), F32),
        in_specs=[hbm] * 6,
        out_specs=pl.BlockSpec(memory_space=pl.ANY),
        scratch_shapes=[
            pltpu.SMEM((GROUPS,), jnp.int32),
            pltpu.SMEM((GROUPS,), F32),
            vmem((LEV, rows, 128), BF16),
            vmem((LEV, rows, 128), F32),
            vmem((2, LEV), F32),
            vmem((ROWS, NLON), F32),
            vmem((GROUPS, 2, LEV), F32),
            vmem((2, ROWS, NLON), F32),
            vmem((CHUNKS, LEV * 8, 256), BF16),
            vmem((CHUNKS, LEV * 8, 256), BF16),
            vmem((256, LEV * 8), BF16),
            vmem((4 * LEV, 256), BF16),
            vmem((256, LEV * 8), BF16),
            vmem((4 * LEV, 384), BF16),
            vmem((EXT, MODES, PADDED), F32),
            vmem((2, EXT - 1, 8, PADDED), F32),
            vmem((ROWS, MODES, WIDE), F32),
            vmem((CHUNKS, 256, 256), BF16),
            vmem((ROWS, MODES, PADDED), I16),
            vmem((1, PADDED), F32),
            vmem((2, ROWS, MODES, PADDED), I16),
            vmem((2, 1, PADDED), F32),
            vmem((4, GLEV, rows, 128), BF16),
            vmem((CHUNKS, 256, 256), BF16),
            vmem((CHUNKS, 4, GLEV, SUB, 128), F32),
            vmem((CHUNKS, 2, GLEV, SUB, 128), I16),
            vmem((CHUNKS, 2, 1, 128), F32),
            vmem((CHUNKS, 2, GLEV, SUB, 128), I16),
            vmem((CHUNKS, 2, 1, 128), F32),
            vmem((CHUNKS, HALF, SUB, 128), I16),
            vmem((CHUNKS, GLEV - HALF, SUB, 128), I16),
            vmem((CHUNKS, 2, 1, 128), F32),
            vmem((CHUNKS, HALF, SUB, 128), I16),
            vmem((CHUNKS, GLEV - HALF, SUB, 128), I16),
            vmem((CHUNKS, 2, 1, 128), F32),
            dma((4 + 2 * CHUNKS,)), dma((CHUNKS,)),
            dma((GROUPS,)), dma((GROUPS,)), dma((2,)), dma((2,)),
            dma((2, MSGS)), dma((2, MSGS)), dma((2, MSGS)), dma((2, MSGS)),
            dma((CHUNKS,)), dma((CHUNKS,)), dma((4,)), dma((4,)),
            dma((2, CHUNKS)), dma((2, CHUNKS)), dma((2, CHUNKS)), dma((2, CHUNKS)),
            dma((2, CHUNKS)), dma((2, CHUNKS)), dma((2, CHUNKS)), dma((2, CHUNKS)),
        ],
        compiler_params=pltpu.CompilerParams(
            collective_id=0, has_side_effects=True, vmem_limit_bytes=53 * 2**20),
    )(*[pltpu.with_memory_space_constraint(a, pltpu.HBM) for a in (tiles(anomalies[0]), tiles(vector), modes, order, weights, diffusivity)])
    return untiles(out)


def solution(mesh):
    return jax.shard_map(
        body,
        mesh=mesh,
        in_specs=(
            P("mode", None, "space", None),
            P(None, "space", None),
            P("mode", None),
            P(),
            P(),
            P("space", None),
        ),
        out_specs=P("mode", "space", None),
        check_vma=False,
    )
```

```python
import jax
import jax.numpy as jnp
from jax import lax
from jax.experimental import pallas as pl
from jax.experimental.pallas import tpu as pltpu
from jax.sharding import PartitionSpec as P

LEV, NLON, DIFF, MODES, ROWS = 136, 2048, 4, 16, 4
GROUPS = 8
GLEV = LEV // GROUPS
TILES = NLON // 128
CHUNKS = 4
SUB = TILES * ROWS // CHUNKS
WIDE = NLON // CHUNKS
PADDED = NLON + 256
EXT = ROWS + 2 * DIFF
UP = (10, 4, 7, 13)
FAR, NEAR, PAST = 0, 1, 2
MSGS = CHUNKS + 1
BY_DISTANCE = (4, 3, 5, 2, 6, 1, 7)
TINY = 1e-33
F32, BF16, I16 = jnp.float32, jnp.bfloat16, jnp.int16


def split(a):
    hi = a.astype(BF16)
    return hi, (a - hi.astype(F32)).astype(BF16)


def pack(a, top):
    return jnp.round(a * (32767.0 / top)).astype(I16)


def kernel(x_hbm, v_hbm, modes_hbm, order_hbm, weights_hbm, diff_hbm, out_ref,
           order_ref, weights_ref, xs, vs, mine, nu, mall, nuext, phi, plo, spread, pick, fwd, bwd, field, face, loc, lcat,
           hq, hsc, hqr, hscr, xsib, lsib, own, zf, zfr, zn, zp, zr, tf, tfr, tn, tnr, tp, tpr,
           lsem, m_s, m_r, d_s, d_r, hq_s, hq_r, hs_s, hs_r, sb_s, sb_r, xb_s, xb_r,
           z_s, z_r, t_s, t_r):
    me = lax.axis_index("mode")
    place = lax.axis_index("space")
    ring, core = me // 2, me % 2
    has_prev = place > 0
    has_next = place < lax.axis_size("space") - 1
    right = {"mode": ((ring + 1) % 4) * 2 + core}
    left = {"mode": ((ring + 3) % 4) * 2 + core}
    partner = {"mode": ring * 2 + 1 - core}
    before, after = {"space": place - 1}, {"space": place + 1}

    def remote(src, dst, ss, rs, dev):
        return pltpu.make_async_remote_copy(
            src_ref=src, dst_ref=dst, send_sem=ss, recv_sem=rs, device_id=dev,
            device_id_type=pl.DeviceIdType.MESH)

    barrier = pltpu.get_barrier_semaphore()

    def greet(dev):
        pl.semaphore_signal(barrier, inc=1, device_id=dev, device_id_type=pl.DeviceIdType.MESH)

    for j in BY_DISTANCE:
        greet({"mode": (me + j) % GROUPS})
    pl.when(has_prev)(lambda: greet(before))
    pl.when(has_next)(lambda: greet(after))

    def chunk_rows(n):
        return pl.ds(pl.multiple_of(n * SUB, SUB), SUB)

    get_modes = pltpu.make_async_copy(modes_hbm, mine, lsem.at[0])
    get_nu = pltpu.make_async_copy(diff_hbm, nu, lsem.at[1])

    def get_x(n):
        return pltpu.make_async_copy(x_hbm.at[:, chunk_rows(n)], xs.at[:, chunk_rows(n)], lsem.at[2 + n])

    def get_v(n):
        return pltpu.make_async_copy(v_hbm.at[:, chunk_rows(n)], vs.at[:, chunk_rows(n)], lsem.at[2 + CHUNKS + n])

    get_order = pltpu.make_async_copy(order_hbm, order_ref, lsem.at[2 + 2 * CHUNKS])
    get_weights = pltpu.make_async_copy(weights_hbm, weights_ref, lsem.at[3 + 2 * CHUNKS])
    for copy in (get_modes, get_nu, get_order, get_weights):
        copy.start()
    for n in range(CHUNKS):
        get_x(n).start()
        get_v(n).start()

    lane_level = lax.broadcasted_iota(jnp.int32, (256, LEV * 8), 1) >> 3
    spread[...] = jnp.where(lane_level == lax.broadcasted_iota(jnp.int32, (256, LEV * 8), 0), 1.0, 0.0).astype(BF16)
    get_modes.wait()
    mall[0] = mine[...]
    get_nu.wait()
    get_order.wait()
    get_weights.wait()

    def products(n):
        get_x(n).wait()
        get_v(n).wait()

        for b in range(LEV // 8):
            lev = slice(b * 8, b * 8 + 8)
            p = xs[lev, chunk_rows(n), :].astype(F32) * vs[lev, chunk_rows(n), :]
            for h in range(2):
                hi, lo = split(p[:, 8 * h : 8 * h + 8, :].reshape(64, 128))
                phi[n, b * 64 : b * 64 + 64, 128 * h : 128 * h + 128] = hi
                plo[n, b * 64 : b * 64 + 64, 128 * h : 128 * h + 128] = lo

    pl.semaphore_wait(barrier, GROUPS - 1 + has_prev.astype(jnp.int32) + has_next.astype(jnp.int32))

    def send_modes(j):
        return remote(mall.at[0], mall.at[j], m_s.at[j], m_r.at[j], {"mode": (me + j) % GROUPS})

    for j in BY_DISTANCE:
        send_modes(j).start()
    nu_up = remote(nu, nuext.at[0], d_s.at[0], d_r.at[0], after)
    nu_down = remote(nu, nuext.at[1], d_s.at[1], d_r.at[1], before)
    pl.when(has_next)(lambda: nu_up.start())
    pl.when(has_prev)(lambda: nu_down.start())

    def run(stage):
        def step(n, carry):
            stage(n)
            return carry
        lax.fori_loop(0, CHUNKS, step, 0)

    def levels_of(i, c):
        return pl.ds((((ring + i) % 4) * 2 + c) * GLEV, GLEV)

    for i in range(4):
        level = (((ring + i) % 4) * 2 + core) * GLEV + (lax.broadcasted_iota(jnp.int32, (LEV, 256), 0) >> 3)
        pick[i * LEV : (i + 1) * LEV, :] = jnp.where(
            lax.broadcasted_iota(jnp.int32, (LEV, 256), 1) == level, 1.0, 0.0).astype(BF16)

    run(products)

    def lend(i):
        return remote(xs.at[levels_of(i, 1 - core)], xsib.at[i], xb_s.at[i], xb_r.at[i], partner)

    for j in range(1, GROUPS):
        send_modes(j).wait_recv()
    modes = jnp.zeros((MODES, LEV), F32)
    for j in range(GROUPS):
        row = lax.broadcasted_iota(jnp.int32, (MODES, LEV), 0) - 2 * ((me - j + GROUPS) % GROUPS)
        modes = jnp.where(row == 0, mall[j, 0:1, :], jnp.where(row == 1, mall[j, 1:2, :], modes))
    modes = jnp.concatenate([modes, jnp.zeros((MODES, 256 - LEV), F32)], axis=1)
    modes_hi, modes_lo = split(modes)

    both = jnp.dot(jnp.concatenate([modes_hi, modes_lo], axis=0), spread[...], preferred_element_type=F32)
    sub = lax.broadcasted_iota(jnp.int32, (MODES, LEV * 8), 1) & 7
    for half in range(2):
        rows = both[half * MODES : (half + 1) * MODES]
        for q in range(8):
            fwd[half * 128 + q * MODES : half * 128 + (q + 1) * MODES, :] = jnp.where(sub == q, rows, 0.0).astype(BF16)

    def peak(a):
        return jnp.maximum(jnp.max(jnp.max(jnp.abs(a), axis=0), axis=0, keepdims=True), TINY)

    def project(n):
        main = jnp.dot(fwd[...], phi[n], preferred_element_type=F32)
        rest = jnp.dot(fwd[0:128, :], plo[n], preferred_element_type=F32)
        total = main[0:128] + main[128:256] + rest
        for par in range(2):
            for r in range(ROWS):
                for h in range(2):
                    at = (1 + 4 * n + 2 * h + par) * 128
                    q = (par * ROWS + r) * MODES
                    field[DIFF + r, :, at : at + 128] = total[q : q + MODES, h * 128 : h * 128 + 128]

    def halo_lanes(i):
        if isinstance(i, int) and i == 0:
            return pl.ds(0, 256)
        return pl.ds(pl.multiple_of(i * WIDE - WIDE + 256, 128), WIDE)

    def halo(i, way):
        lanes = halo_lanes(i)
        dev = after if way == 0 else before
        return (remote(hq.at[:, :, lanes], hqr.at[way, :, :, lanes], hq_s.at[way, i], hq_r.at[way, i], dev),
                remote(hsc.at[:, lanes], hscr.at[way, :, lanes], hs_s.at[way, i], hs_r.at[way, i], dev))

    def each(copies, what):
        for copy in copies:
            getattr(copy, what)()

    def send_halo(i):
        lanes = halo_lanes(i)
        u = field[DIFF : DIFF + ROWS, :, lanes]
        top = peak(u)
        hsc[:, lanes] = top * (1.0 / 32767.0)
        hq[:, :, lanes] = pack(u, top[None])
        pl.when(has_next)(lambda: each(halo(i, 0), "start"))
        pl.when(has_prev)(lambda: each(halo(i, 1), "start"))

    own_rows = slice(DIFF, DIFF + ROWS)
    project(3)
    field[own_rows, :, 0:128] = field[own_rows, :, NLON : NLON + 128]
    project(0)
    field[own_rows, :, NLON + 128 : PADDED] = field[own_rows, :, 128:256]
    send_halo(0)
    project(1)
    send_halo(1)
    project(2)
    for i in range(2, MSGS):
        send_halo(i)

    for i in range(4):
        lend(i).start()

    rep_hi = jnp.concatenate([modes_hi] * 8, axis=0)
    rep_lo = jnp.concatenate([modes_lo] * 8, axis=0)
    same = (lax.broadcasted_iota(jnp.int32, (4 * LEV, 128), 0) & 7) == (lax.broadcasted_iota(jnp.int32, (4 * LEV, 128), 1) >> 4)
    last = (((1,), (1,)), ((), ()))
    hi = jnp.where(same, lax.dot_general(pick[...], rep_hi, last, preferred_element_type=F32), 0.0).astype(BF16)
    bwd[:, 0:128] = hi
    bwd[:, 128:256] = hi
    lo = lax.dot_general(pick[...], rep_lo, last, preferred_element_type=F32)
    bwd[:, 256:384] = jnp.where(same, lo, 0.0).astype(BF16)

    @pl.when(has_prev)
    def _():
        nu_up.wait_recv()

    @pl.when(has_next)
    def _():
        nu_down.wait_recv()

    @pl.when(jnp.logical_not(has_prev))
    def _():
        nuext[0] = jnp.zeros((ROWS, NLON), F32)
        field[0:DIFF] = jnp.zeros((DIFF, MODES, PADDED), F32)

    @pl.when(jnp.logical_not(has_next))
    def _():
        nuext[1] = jnp.zeros((ROWS, NLON), F32)
        field[DIFF + ROWS : EXT] = jnp.zeros((DIFF, MODES, PADDED), F32)

    def nu_row(a):
        src = nuext[0] if a < DIFF else nu[...] if a < DIFF + ROWS else nuext[1]
        r = a % ROWS
        return jnp.broadcast_to(src[r : r + 1, :], (8, NLON))

    for a in range(EXT - 1):
        here = nu_row(a)
        for c, other in enumerate((pltpu.roll(here, NLON - 1, 1), nu_row(a + 1))):
            arm = 0.5 * (here + other)
            face[c, a, :, 128 : NLON + 128] = arm
            face[c, a, :, 0:128] = arm[:, NLON - 128 : NLON]
            face[c, a, :, NLON + 128 : PADDED] = arm[:, 0:128]

    weight = jnp.float32(0.0)
    for s in range(GROUPS):
        weight = weight + jnp.where(order_ref[s] == me, weights_ref[s], 0.0)

    def take_halo(i):
        lanes = halo_lanes(i)

        @pl.when(has_prev)
        def _():
            each(halo(i, 0), "wait_recv")
            field[0:DIFF, :, lanes] = hqr[0, :, :, lanes].astype(F32) * hscr[0, :, lanes][None]

        @pl.when(has_next)
        def _():
            each(halo(i, 1), "wait_recv")
            field[DIFF + ROWS : EXT, :, lanes] = hqr[1, :, :, lanes].astype(F32) * hscr[1, :, lanes][None]

    window = WIDE + 256
    top_mask, low_mask = has_prev.astype(F32), has_next.astype(F32)

    def diffuse(n):
        lanes = pl.ds(pl.multiple_of(n * WIDE, 128), window)
        def both_halves(c, a):
            arm = face[c, a, :, lanes]
            return jnp.concatenate([arm, arm], axis=0)

        u = [field[a, :, lanes] for a in range(EXT)]
        for s in range(1, DIFF + 1):
            new = []
            north = both_halves(1, s - 1) * (u[1] - u[0])
            for a in range(s, EXT - s):
                c, down = u[a - s + 1], u[a - s + 2]
                south = both_halves(1, a) * (down - c)
                east = both_halves(0, a) * (pltpu.roll(c, window - 1, 1) - c)
                total = c + (south - north) + (east - pltpu.roll(east, 1, 1))
                if a < DIFF:
                    total = total * top_mask
                elif a >= DIFF + ROWS:
                    total = total * low_mask
                new.append(total)
                north = south
            u = new
        for r in range(ROWS):
            loc[r] = weight * u[r][:, 128 : 128 + WIDE]
        for par in range(2):
            for r in range(ROWS):
                q = (par * ROWS + r) * MODES
                for h in range(2):
                    t = (2 * h + par) * 128
                    hi, lo = split(loc[r, :, t : t + 128])
                    cols = slice(h * 128, h * 128 + 128)
                    lcat[n, q : q + MODES, cols] = hi
                    lcat[n, 128 + q : 128 + q + MODES, cols] = lo

    def share(n):
        return remote(lcat.at[n], lsib.at[n], sb_s.at[n], sb_r.at[n], partner)

    def backward(terms):
        return (jnp.dot(bwd[:, 0:256], terms[...], preferred_element_type=F32)
                + jnp.dot(bwd[:, 256:384], terms[0:128, :], preferred_element_type=F32))

    def times(back, i, x):
        return jnp.concatenate(
            [x[:, 8 * h : 8 * h + 8, :] * back[i * LEV : (i + 1) * LEV, h * 128 : h * 128 + 128].reshape(GLEV, 8, 128)
             for h in range(2)], axis=1)

    def carry_sum(kind, n, way, c):
        dest = (c + 2) % 4 if kind == FAR else (c + 1) % 4 if way == 0 else (c + 3) % 4
        rising = (way == 0) == (kind != NEAR)
        cut = slice(0, UP[dest]) if rising else slice(UP[dest], GLEV)
        dev = right if way == 0 else left
        if kind == FAR:
            src, dst, one, two = zf.at[n, cut], zfr.at[n, way, cut], tf.at[n], tfr.at[n, way]
        elif kind == NEAR:
            src, dst, one, two = zn.at[n, way, cut], zr.at[n, way, cut], tn.at[n, way], tnr.at[n, way]
        else:
            src, dst, one, two = zp.at[n, way, cut], zr.at[n, way, cut], tp.at[n, way], tpr.at[n, way]
        return (remote(src, dst, z_s.at[kind, way, n], z_r.at[kind, way, n], dev),
                remote(one, two, t_s.at[kind, way, n], t_r.at[kind, way, n], dev))

    def act(kind, n, way, what):
        step = 0 if what != "wait_recv" else 3 if way == 0 else 1
        for c in range(4):
            pl.when(ring == c)(lambda c=c: each(carry_sum(kind, n, way, (c + step) % 4), what))

    lev_index = lax.broadcasted_iota(jnp.int32, (GLEV, 1, 128), 0)

    def rises(step):
        dest = (ring + step) % 4
        up = jnp.int32(UP[0])
        for d in range(1, 4):
            up = jnp.where(dest == d, UP[d], up)
        return lev_index < up

    def quantize(a, q, t):
        top = peak(a)
        t[...] = top * (1.0 / 32767.0)
        q[...] = pack(a, top[None])

    def stage_a(n):
        take_halo(n + 1)
        diffuse(n)
        share(n).start()
        back = backward(lcat.at[n])
        for i in range(4):
            own[n, i] = times(back, i, xs[levels_of(i, core), chunk_rows(n), :].astype(F32))

    def stage_b(n):
        share(n).wait_recv()
        back = backward(lsib.at[n])

        def both(i):
            return own[n, i] + times(back, i, xsib[i, :, chunk_rows(n), :].astype(F32))

        quantize(both(2), zf.at[n], tf.at[n])
        for way in range(2):
            act(FAR, n, way, "start")
        for way in range(2):
            i = 1 if way == 0 else 3
            own[n, i] = both(i)
            quantize(own[n, i], zn.at[n, way], tn.at[n, way])
        pl.when(n == 0)(lambda: start_near(n))
        own[n, 0] = both(0)

    def start_near(n):
        for way in range(2):
            act(NEAR, n, way, "start")

    def stage_c(n):
        for way in range(2):
            act(FAR, n, way, "wait_recv")
            got = own[n, 1 if way == 0 else 3] + zfr[n, way].astype(F32) * tfr[n, way][None]
            up = rises(1 if way == 0 else 3)
            a = jnp.where(up, got, 0.0) if way == 0 else jnp.where(up, 0.0, got)
            quantize(a, zp.at[n, way], tp.at[n, way])
            act(PAST, n, way, "start")

    def stage_d(n):
        total = own[n, 0]
        up = rises(0)
        for way in range(2):
            act(NEAR, n, way, "wait_recv")
            act(PAST, n, way, "wait_recv")
            scale = jnp.where(up if way == 0 else jnp.logical_not(up), tpr[n, way][None], tnr[n, way][None])
            total = total + zr[n, way].astype(F32) * scale
        out_ref[:, chunk_rows(n), :] = total

    take_halo(0)
    for i in range(4):
        lend(i).wait_recv()

    def pipe(it, carry):
        pl.when(it < CHUNKS)(lambda: stage_a(it))
        pl.when(it != 1)(lambda: stage_b(jnp.maximum(it - 1, 0)))
        return carry

    def later_near(n, carry):
        start_near(n)
        return carry

    lax.fori_loop(0, CHUNKS + 1, pipe, 0)
    lax.fori_loop(1, CHUNKS, later_near, 0)
    run(stage_c)
    run(stage_d)

    for j in range(1, GROUPS):
        send_modes(j).wait_send()
    for i in range(4):
        lend(i).wait_send()

    @pl.when(has_next)
    def _():
        nu_up.wait_send()
        for i in range(MSGS):
            each(halo(i, 0), "wait_send")

    @pl.when(has_prev)
    def _():
        nu_down.wait_send()
        for i in range(MSGS):
            each(halo(i, 1), "wait_send")

    def sent(n):
        share(n).wait_send()
        for way in range(2):
            for kind in (FAR, NEAR, PAST):
                act(kind, n, way, "wait_send")

    run(sent)


def tiles(a):
    lev = a.shape[0]
    return a.reshape(lev, ROWS, TILES, 128).transpose(0, 2, 1, 3).reshape(lev, TILES * ROWS, 128)


def untiles(a):
    lev = a.shape[0]
    return a.reshape(lev, TILES, ROWS, 128).transpose(0, 2, 1, 3).reshape(lev, ROWS, NLON)


def body(anomalies, vector, modes, order, weights, diffusivity):
    vmem, dma = pltpu.VMEM, pltpu.SemaphoreType.DMA
    hbm = pl.BlockSpec(memory_space=pltpu.HBM)
    rows = TILES * ROWS
    out = pl.pallas_call(
        kernel,
        out_shape=jax.ShapeDtypeStruct((GLEV, rows, 128), F32),
        in_specs=[hbm] * 6,
        out_specs=pl.BlockSpec(memory_space=pltpu.VMEM),
        scratch_shapes=[
            pltpu.SMEM((GROUPS,), jnp.int32),
            pltpu.SMEM((GROUPS,), F32),
            vmem((LEV, rows, 128), BF16),
            vmem((LEV, rows, 128), F32),
            vmem((2, LEV), F32),
            vmem((ROWS, NLON), F32),
            vmem((GROUPS, 2, LEV), F32),
            vmem((2, ROWS, NLON), F32),
            vmem((CHUNKS, LEV * 8, 256), BF16),
            vmem((CHUNKS, LEV * 8, 256), BF16),
            vmem((256, LEV * 8), BF16),
            vmem((4 * LEV, 256), BF16),
            vmem((256, LEV * 8), BF16),
            vmem((4 * LEV, 384), BF16),
            vmem((EXT, MODES, PADDED), F32),
            vmem((2, EXT - 1, 8, PADDED), F32),
            vmem((ROWS, MODES, WIDE), F32),
            vmem((CHUNKS, 256, 256), BF16),
            vmem((ROWS, MODES, PADDED), I16),
            vmem((1, PADDED), F32),
            vmem((2, ROWS, MODES, PADDED), I16),
            vmem((2, 1, PADDED), F32),
            vmem((4, GLEV, rows, 128), BF16),
            vmem((CHUNKS, 256, 256), BF16),
            vmem((CHUNKS, 4, GLEV, SUB, 128), F32),
            vmem((CHUNKS, GLEV, SUB, 128), I16),
            vmem((CHUNKS, 2, GLEV, SUB, 128), I16),
            vmem((CHUNKS, 2, GLEV, SUB, 128), I16),
            vmem((CHUNKS, 2, GLEV, SUB, 128), I16),
            vmem((CHUNKS, 2, GLEV, SUB, 128), I16),
            vmem((CHUNKS, 1, 128), F32),
            vmem((CHUNKS, 2, 1, 128), F32),
            vmem((CHUNKS, 2, 1, 128), F32),
            vmem((CHUNKS, 2, 1, 128), F32),
            vmem((CHUNKS, 2, 1, 128), F32),
            vmem((CHUNKS, 2, 1, 128), F32),
            dma((4 + 2 * CHUNKS,)),
            dma((GROUPS,)), dma((GROUPS,)), dma((2,)), dma((2,)),
            dma((2, MSGS)), dma((2, MSGS)), dma((2, MSGS)), dma((2, MSGS)),
            dma((CHUNKS,)), dma((CHUNKS,)), dma((4,)), dma((4,)),
            dma((3, 2, CHUNKS)), dma((3, 2, CHUNKS)), dma((3, 2, CHUNKS)), dma((3, 2, CHUNKS)),
        ],
        compiler_params=pltpu.CompilerParams(
            collective_id=0, has_side_effects=True, vmem_limit_bytes=53 * 2**20),
    )(*[pltpu.with_memory_space_constraint(a, pltpu.HBM) for a in (tiles(anomalies[0]), tiles(vector), modes, order, weights, diffusivity)])
    return untiles(out)


def solution(mesh):
    return jax.shard_map(
        body,
        mesh=mesh,
        in_specs=(
            P("mode", None, "space", None),
            P(None, "space", None),
            P("mode", None),
            P(),
            P(),
            P("space", None),
        ),
        out_specs=P("mode", "space", None),
        check_vma=False,
    )
```

```python
import jax
import jax.numpy as jnp
from jax import lax
from jax.experimental import pallas as pl
from jax.experimental.pallas import tpu as pltpu
from jax.sharding import PartitionSpec as P

LEV, NLON, DIFF, MODES, ROWS = 136, 2048, 4, 16, 4
GROUPS = 8
GLEV = LEV // GROUPS
TILES = NLON // 128
CHUNKS = 4
SUB = TILES * ROWS // CHUNKS
WIDE = NLON // CHUNKS
PADDED = NLON + 256
EXT = ROWS + 2 * DIFF
UP = (10, 5, 7, 12)
FAR, NEAR, PAST = 0, 1, 2
MSGS = CHUNKS + 1
BY_DISTANCE = (4, 3, 5, 2, 6, 1, 7)
TINY = 1e-33
F32, BF16, I16 = jnp.float32, jnp.bfloat16, jnp.int16


def split(a):
    hi = a.astype(BF16)
    return hi, (a - hi.astype(F32)).astype(BF16)


def pack(a, top):
    return jnp.round(a * (32767.0 / top)).astype(I16)


def kernel(x_hbm, v_hbm, modes_hbm, order_hbm, weights_hbm, diff_hbm, out_ref,
           order_ref, weights_ref, xs, vs, mine, nu, mall, nuext, phi, plo, spread, pick, fwd, bwd, field, face, loc, lcat,
           hq, hsc, hqr, hscr, xsib, lsib, own, zf, zfr, zn, zp, zr, tf, tfr, tn, tnr, tp, tpr,
           lsem, m_s, m_r, d_s, d_r, hq_s, hq_r, hs_s, hs_r, sb_s, sb_r, xb_s, xb_r,
           z_s, z_r, t_s, t_r):
    me = lax.axis_index("mode")
    place = lax.axis_index("space")
    ring, core = me // 2, me % 2
    has_prev = place > 0
    has_next = place < lax.axis_size("space") - 1
    right = {"mode": ((ring + 1) % 4) * 2 + core}
    left = {"mode": ((ring + 3) % 4) * 2 + core}
    partner = {"mode": ring * 2 + 1 - core}
    before, after = {"space": place - 1}, {"space": place + 1}

    def remote(src, dst, ss, rs, dev):
        return pltpu.make_async_remote_copy(
            src_ref=src, dst_ref=dst, send_sem=ss, recv_sem=rs, device_id=dev,
            device_id_type=pl.DeviceIdType.MESH)

    barrier = pltpu.get_barrier_semaphore()

    def greet(dev):
        pl.semaphore_signal(barrier, inc=1, device_id=dev, device_id_type=pl.DeviceIdType.MESH)

    for j in BY_DISTANCE:
        greet({"mode": (me + j) % GROUPS})
    pl.when(has_prev)(lambda: greet(before))
    pl.when(has_next)(lambda: greet(after))

    def chunk_rows(n):
        return pl.ds(pl.multiple_of(n * SUB, SUB), SUB)

    get_modes = pltpu.make_async_copy(modes_hbm, mine, lsem.at[0])
    get_nu = pltpu.make_async_copy(diff_hbm, nu, lsem.at[1])

    def get_x(n):
        return pltpu.make_async_copy(x_hbm.at[:, chunk_rows(n)], xs.at[:, chunk_rows(n)], lsem.at[2 + n])

    def get_v(n):
        return pltpu.make_async_copy(v_hbm.at[:, chunk_rows(n)], vs.at[:, chunk_rows(n)], lsem.at[2 + CHUNKS + n])

    get_order = pltpu.make_async_copy(order_hbm, order_ref, lsem.at[2 + 2 * CHUNKS])
    get_weights = pltpu.make_async_copy(weights_hbm, weights_ref, lsem.at[3 + 2 * CHUNKS])
    for copy in (get_modes, get_nu, get_order, get_weights):
        copy.start()
    for n in range(CHUNKS):
        get_x(n).start()
        get_v(n).start()

    lane_level = lax.broadcasted_iota(jnp.int32, (256, LEV * 8), 1) >> 3
    spread[...] = jnp.where(lane_level == lax.broadcasted_iota(jnp.int32, (256, LEV * 8), 0), 1.0, 0.0).astype(BF16)
    get_modes.wait()
    mall[0] = mine[...]
    get_nu.wait()
    get_order.wait()
    get_weights.wait()

    def products(n):
        get_x(n).wait()
        get_v(n).wait()

        for b in range(LEV // 8):
            lev = slice(b * 8, b * 8 + 8)
            p = xs[lev, chunk_rows(n), :].astype(F32) * vs[lev, chunk_rows(n), :]
            for h in range(2):
                hi, lo = split(p[:, 8 * h : 8 * h + 8, :].reshape(64, 128))
                phi[n, b * 64 : b * 64 + 64, 128 * h : 128 * h + 128] = hi
                plo[n, b * 64 : b * 64 + 64, 128 * h : 128 * h + 128] = lo

    pl.semaphore_wait(barrier, GROUPS - 1 + has_prev.astype(jnp.int32) + has_next.astype(jnp.int32))

    def send_modes(j):
        return remote(mall.at[0], mall.at[j], m_s.at[j], m_r.at[j], {"mode": (me + j) % GROUPS})

    for j in BY_DISTANCE:
        send_modes(j).start()
    nu_up = remote(nu, nuext.at[0], d_s.at[0], d_r.at[0], after)
    nu_down = remote(nu, nuext.at[1], d_s.at[1], d_r.at[1], before)
    pl.when(has_next)(lambda: nu_up.start())
    pl.when(has_prev)(lambda: nu_down.start())

    def run(stage):
        def step(n, carry):
            stage(n)
            return carry
        lax.fori_loop(0, CHUNKS, step, 0)

    def levels_of(i, c):
        return pl.ds((((ring + i) % 4) * 2 + c) * GLEV, GLEV)

    for i in range(4):
        level = (((ring + i) % 4) * 2 + core) * GLEV + (lax.broadcasted_iota(jnp.int32, (LEV, 256), 0) >> 3)
        pick[i * LEV : (i + 1) * LEV, :] = jnp.where(
            lax.broadcasted_iota(jnp.int32, (LEV, 256), 1) == level, 1.0, 0.0).astype(BF16)

    run(products)

    def lend(i):
        return remote(xs.at[levels_of(i, 1 - core)], xsib.at[i], xb_s.at[i], xb_r.at[i], partner)

    for j in range(1, GROUPS):
        send_modes(j).wait_recv()
    modes = jnp.zeros((MODES, LEV), F32)
    for j in range(GROUPS):
        row = lax.broadcasted_iota(jnp.int32, (MODES, LEV), 0) - 2 * ((me - j + GROUPS) % GROUPS)
        modes = jnp.where(row == 0, mall[j, 0:1, :], jnp.where(row == 1, mall[j, 1:2, :], modes))
    modes = jnp.concatenate([modes, jnp.zeros((MODES, 256 - LEV), F32)], axis=1)
    modes_hi, modes_lo = split(modes)

    both = jnp.dot(jnp.concatenate([modes_hi, modes_lo], axis=0), spread[...], preferred_element_type=F32)
    sub = lax.broadcasted_iota(jnp.int32, (MODES, LEV * 8), 1) & 7
    for half in range(2):
        rows = both[half * MODES : (half + 1) * MODES]
        for q in range(8):
            fwd[half * 128 + q * MODES : half * 128 + (q + 1) * MODES, :] = jnp.where(sub == q, rows, 0.0).astype(BF16)

    def peak(a):
        return jnp.maximum(jnp.max(jnp.max(jnp.abs(a), axis=0), axis=0, keepdims=True), TINY)

    def project(n):
        main = jnp.dot(fwd[...], phi[n], preferred_element_type=F32)
        rest = jnp.dot(fwd[0:128, :], plo[n], preferred_element_type=F32)
        total = main[0:128] + main[128:256] + rest
        for par in range(2):
            for r in range(ROWS):
                for h in range(2):
                    at = (1 + 4 * n + 2 * h + par) * 128
                    q = (par * ROWS + r) * MODES
                    field[DIFF + r, :, at : at + 128] = total[q : q + MODES, h * 128 : h * 128 + 128]

    def halo_lanes(i):
        if isinstance(i, int) and i == 0:
            return pl.ds(0, 256)
        return pl.ds(pl.multiple_of(i * WIDE - WIDE + 256, 128), WIDE)

    def halo(i, way):
        lanes = halo_lanes(i)
        dev = after if way == 0 else before
        return (remote(hq.at[:, :, lanes], hqr.at[way, :, :, lanes], hq_s.at[way, i], hq_r.at[way, i], dev),
                remote(hsc.at[:, lanes], hscr.at[way, :, lanes], hs_s.at[way, i], hs_r.at[way, i], dev))

    def each(copies, what):
        for copy in copies:
            getattr(copy, what)()

    def send_halo(i):
        lanes = halo_lanes(i)
        u = field[DIFF : DIFF + ROWS, :, lanes]
        top = peak(u)
        hsc[:, lanes] = top * (1.0 / 32767.0)
        hq[:, :, lanes] = pack(u, top[None])
        pl.when(has_next)(lambda: each(halo(i, 0), "start"))
        pl.when(has_prev)(lambda: each(halo(i, 1), "start"))

    own_rows = slice(DIFF, DIFF + ROWS)
    project(3)
    field[own_rows, :, 0:128] = field[own_rows, :, NLON : NLON + 128]
    project(0)
    field[own_rows, :, NLON + 128 : PADDED] = field[own_rows, :, 128:256]
    send_halo(0)
    project(1)
    send_halo(1)
    project(2)
    for i in range(2, MSGS):
        send_halo(i)

    for i in range(4):
        lend(i).start()

    rep_hi = jnp.concatenate([modes_hi] * 8, axis=0)
    rep_lo = jnp.concatenate([modes_lo] * 8, axis=0)
    same = (lax.broadcasted_iota(jnp.int32, (4 * LEV, 128), 0) & 7) == (lax.broadcasted_iota(jnp.int32, (4 * LEV, 128), 1) >> 4)
    last = (((1,), (1,)), ((), ()))
    hi = jnp.where(same, lax.dot_general(pick[...], rep_hi, last, preferred_element_type=F32), 0.0).astype(BF16)
    bwd[:, 0:128] = hi
    bwd[:, 128:256] = hi
    lo = lax.dot_general(pick[...], rep_lo, last, preferred_element_type=F32)
    bwd[:, 256:384] = jnp.where(same, lo, 0.0).astype(BF16)

    @pl.when(has_prev)
    def _():
        nu_up.wait_recv()

    @pl.when(has_next)
    def _():
        nu_down.wait_recv()

    @pl.when(jnp.logical_not(has_prev))
    def _():
        nuext[0] = jnp.zeros((ROWS, NLON), F32)
        field[0:DIFF] = jnp.zeros((DIFF, MODES, PADDED), F32)

    @pl.when(jnp.logical_not(has_next))
    def _():
        nuext[1] = jnp.zeros((ROWS, NLON), F32)
        field[DIFF + ROWS : EXT] = jnp.zeros((DIFF, MODES, PADDED), F32)

    def nu_row(a):
        src = nuext[0] if a < DIFF else nu[...] if a < DIFF + ROWS else nuext[1]
        r = a % ROWS
        return jnp.broadcast_to(src[r : r + 1, :], (8, NLON))

    for a in range(EXT - 1):
        here = nu_row(a)
        for c, other in enumerate((pltpu.roll(here, NLON - 1, 1), nu_row(a + 1))):
            arm = 0.5 * (here + other)
            face[c, a, :, 128 : NLON + 128] = arm
            face[c, a, :, 0:128] = arm[:, NLON - 128 : NLON]
            face[c, a, :, NLON + 128 : PADDED] = arm[:, 0:128]

    weight = jnp.float32(0.0)
    for s in range(GROUPS):
        weight = weight + jnp.where(order_ref[s] == me, weights_ref[s], 0.0)

    def take_halo(i):
        lanes = halo_lanes(i)

        @pl.when(has_prev)
        def _():
            each(halo(i, 0), "wait_recv")
            field[0:DIFF, :, lanes] = hqr[0, :, :, lanes].astype(F32) * hscr[0, :, lanes][None]

        @pl.when(has_next)
        def _():
            each(halo(i, 1), "wait_recv")
            field[DIFF + ROWS : EXT, :, lanes] = hqr[1, :, :, lanes].astype(F32) * hscr[1, :, lanes][None]

    window = WIDE + 256
    top_mask, low_mask = has_prev.astype(F32), has_next.astype(F32)

    def diffuse(n):
        lanes = pl.ds(pl.multiple_of(n * WIDE, 128), window)
        for kh in range(2):
            ks = slice(kh * 8, kh * 8 + 8)
            levels = [{} for _ in range(DIFF + 1)]
            souths = [{} for _ in range(DIFF + 1)]

            def cell(s, a):
                return field[a, ks, lanes] if s == 0 else levels[s][a]

            def south_of(s, a):
                if a not in souths[s]:
                    souths[s][a] = face[1, a, :, lanes] * (cell(s, a + 1) - cell(s, a))
                return souths[s][a]

            for t in range(1, EXT + 2 * DIFF):
                for s in range(1, DIFF + 1):
                    a = t - 2 * (s - 1) + (s - 1)
                    if s <= a < EXT - s:
                        c = cell(s - 1, a)
                        east = face[0, a, :, lanes] * (pltpu.roll(c, window - 1, 1) - c)
                        total = c + (south_of(s - 1, a) - south_of(s - 1, a - 1)) + (east - pltpu.roll(east, 1, 1))
                        if a < DIFF:
                            total = total * top_mask
                        elif a >= DIFF + ROWS:
                            total = total * low_mask
                        levels[s][a] = total
            for r in range(ROWS):
                loc[r, ks, :] = weight * levels[DIFF][DIFF + r][:, 128 : 128 + WIDE]
        for par in range(2):
            for r in range(ROWS):
                q = (par * ROWS + r) * MODES
                for h in range(2):
                    t = (2 * h + par) * 128
                    hi, lo = split(loc[r, :, t : t + 128])
                    cols = slice(h * 128, h * 128 + 128)
                    lcat[n, q : q + MODES, cols] = hi
                    lcat[n, 128 + q : 128 + q + MODES, cols] = lo

    def share(n):
        return remote(lcat.at[n], lsib.at[n], sb_s.at[n], sb_r.at[n], partner)

    def backward(terms):
        return (jnp.dot(bwd[:, 0:256], terms[...], preferred_element_type=F32)
                + jnp.dot(bwd[:, 256:384], terms[0:128, :], preferred_element_type=F32))

    def times(back, i, x):
        return jnp.concatenate(
            [x[:, 8 * h : 8 * h + 8, :] * back[i * LEV : (i + 1) * LEV, h * 128 : h * 128 + 128].reshape(GLEV, 8, 128)
             for h in range(2)], axis=1)

    def carry_sum(kind, n, way, c):
        dest = (c + 2) % 4 if kind == FAR else (c + 1) % 4 if way == 0 else (c + 3) % 4
        rising = (way == 0) == (kind != NEAR)
        cut = slice(0, UP[dest]) if rising else slice(UP[dest], GLEV)
        dev = right if way == 0 else left
        if kind == FAR:
            src, dst, one, two = zf.at[n, cut], zfr.at[n, way, cut], tf.at[n], tfr.at[n, way]
        elif kind == NEAR:
            src, dst, one, two = zn.at[n, way, cut], zr.at[n, way, cut], tn.at[n, way], tnr.at[n, way]
        else:
            src, dst, one, two = zp.at[n, way, cut], zr.at[n, way, cut], tp.at[n, way], tpr.at[n, way]
        return (remote(src, dst, z_s.at[kind, way, n], z_r.at[kind, way, n], dev),
                remote(one, two, t_s.at[kind, way, n], t_r.at[kind, way, n], dev))

    def act(kind, n, way, what):
        step = 0 if what != "wait_recv" else 3 if way == 0 else 1
        for c in range(4):
            pl.when(ring == c)(lambda c=c: each(carry_sum(kind, n, way, (c + step) % 4), what))

    lev_index = lax.broadcasted_iota(jnp.int32, (GLEV, 1, 128), 0)

    def rises(step):
        dest = (ring + step) % 4
        up = jnp.int32(UP[0])
        for d in range(1, 4):
            up = jnp.where(dest == d, UP[d], up)
        return lev_index < up

    def quantize(a, q, t):
        top = peak(a)
        t[...] = top * (1.0 / 32767.0)
        q[...] = pack(a, top[None])

    def stage_a(n):
        take_halo(n + 1)
        diffuse(n)
        share(n).start()
        back = backward(lcat.at[n])
        for i in range(4):
            own[n, i] = times(back, i, xs[levels_of(i, core), chunk_rows(n), :].astype(F32))

    def stage_b(n):
        share(n).wait_recv()
        back = backward(lsib.at[n])

        def both(i):
            return own[n, i] + times(back, i, xsib[i, :, chunk_rows(n), :].astype(F32))

        quantize(both(2), zf.at[n], tf.at[n])
        for way in range(2):
            act(FAR, n, way, "start")
        for way in range(2):
            i = 1 if way == 0 else 3
            own[n, i] = both(i)
            quantize(own[n, i], zn.at[n, way], tn.at[n, way])
        pl.when(n < 2)(lambda: start_near(n))
        own[n, 0] = both(0)

    def start_near(n):
        for way in range(2):
            act(NEAR, n, way, "start")

    def stage_c(n):
        for way in range(2):
            act(FAR, n, way, "wait_recv")
            got = own[n, 1 if way == 0 else 3] + zfr[n, way].astype(F32) * tfr[n, way][None]
            up = rises(1 if way == 0 else 3)
            a = jnp.where(up, got, 0.0) if way == 0 else jnp.where(up, 0.0, got)
            quantize(a, zp.at[n, way], tp.at[n, way])
            act(PAST, n, way, "start")

    def stage_d(n):
        total = own[n, 0]
        up = rises(0)
        for way in range(2):
            act(NEAR, n, way, "wait_recv")
            act(PAST, n, way, "wait_recv")
            scale = jnp.where(up if way == 0 else jnp.logical_not(up), tpr[n, way][None], tnr[n, way][None])
            total = total + zr[n, way].astype(F32) * scale
        out_ref[:, chunk_rows(n), :] = total

    take_halo(0)
    for i in range(4):
        lend(i).wait_recv()

    def pipe(it, carry):
        pl.when(it < CHUNKS)(lambda: stage_a(it))
        pl.when(it != 1)(lambda: stage_b(jnp.maximum(it - 1, 0)))
        return carry

    def later_near(n, carry):
        start_near(n)
        return carry

    lax.fori_loop(0, CHUNKS + 1, pipe, 0)
    lax.fori_loop(2, CHUNKS, later_near, 0)
    run(stage_c)
    run(stage_d)

    for j in range(1, GROUPS):
        send_modes(j).wait_send()
    for i in range(4):
        lend(i).wait_send()

    @pl.when(has_next)
    def _():
        nu_up.wait_send()
        for i in range(MSGS):
            each(halo(i, 0), "wait_send")

    @pl.when(has_prev)
    def _():
        nu_down.wait_send()
        for i in range(MSGS):
            each(halo(i, 1), "wait_send")

    def sent(n):
        share(n).wait_send()
        for way in range(2):
            for kind in (FAR, NEAR, PAST):
                act(kind, n, way, "wait_send")

    run(sent)


def tiles(a):
    lev = a.shape[0]
    return a.reshape(lev, ROWS, TILES, 128).transpose(0, 2, 1, 3).reshape(lev, TILES * ROWS, 128)


def untiles(a):
    lev = a.shape[0]
    return a.reshape(lev, TILES, ROWS, 128).transpose(0, 2, 1, 3).reshape(lev, ROWS, NLON)


def body(anomalies, vector, modes, order, weights, diffusivity):
    vmem, dma = pltpu.VMEM, pltpu.SemaphoreType.DMA
    hbm = pl.BlockSpec(memory_space=pltpu.HBM)
    rows = TILES * ROWS
    out = pl.pallas_call(
        kernel,
        out_shape=jax.ShapeDtypeStruct((GLEV, rows, 128), F32),
        in_specs=[hbm] * 6,
        out_specs=pl.BlockSpec(memory_space=pltpu.VMEM),
        scratch_shapes=[
            pltpu.SMEM((GROUPS,), jnp.int32),
            pltpu.SMEM((GROUPS,), F32),
            vmem((LEV, rows, 128), BF16),
            vmem((LEV, rows, 128), F32),
            vmem((2, LEV), F32),
            vmem((ROWS, NLON), F32),
            vmem((GROUPS, 2, LEV), F32),
            vmem((2, ROWS, NLON), F32),
            vmem((CHUNKS, LEV * 8, 256), BF16),
            vmem((CHUNKS, LEV * 8, 256), BF16),
            vmem((256, LEV * 8), BF16),
            vmem((4 * LEV, 256), BF16),
            vmem((256, LEV * 8), BF16),
            vmem((4 * LEV, 384), BF16),
            vmem((EXT, MODES, PADDED), F32),
            vmem((2, EXT - 1, 8, PADDED), F32),
            vmem((ROWS, MODES, WIDE), F32),
            vmem((CHUNKS, 256, 256), BF16),
            vmem((ROWS, MODES, PADDED), I16),
            vmem((1, PADDED), F32),
            vmem((2, ROWS, MODES, PADDED), I16),
            vmem((2, 1, PADDED), F32),
            vmem((4, GLEV, rows, 128), BF16),
            vmem((CHUNKS, 256, 256), BF16),
            vmem((CHUNKS, 4, GLEV, SUB, 128), F32),
            vmem((CHUNKS, GLEV, SUB, 128), I16),
            vmem((CHUNKS, 2, GLEV, SUB, 128), I16),
            vmem((CHUNKS, 2, GLEV, SUB, 128), I16),
            vmem((CHUNKS, 2, GLEV, SUB, 128), I16),
            vmem((CHUNKS, 2, GLEV, SUB, 128), I16),
            vmem((CHUNKS, 1, 128), F32),
            vmem((CHUNKS, 2, 1, 128), F32),
            vmem((CHUNKS, 2, 1, 128), F32),
            vmem((CHUNKS, 2, 1, 128), F32),
            vmem((CHUNKS, 2, 1, 128), F32),
            vmem((CHUNKS, 2, 1, 128), F32),
            dma((4 + 2 * CHUNKS,)),
            dma((GROUPS,)), dma((GROUPS,)), dma((2,)), dma((2,)),
            dma((2, MSGS)), dma((2, MSGS)), dma((2, MSGS)), dma((2, MSGS)),
            dma((CHUNKS,)), dma((CHUNKS,)), dma((4,)), dma((4,)),
            dma((3, 2, CHUNKS)), dma((3, 2, CHUNKS)), dma((3, 2, CHUNKS)), dma((3, 2, CHUNKS)),
        ],
        compiler_params=pltpu.CompilerParams(
            collective_id=0, has_side_effects=True, vmem_limit_bytes=53 * 2**20),
    )(*[pltpu.with_memory_space_constraint(a, pltpu.HBM) for a in (tiles(anomalies[0]), tiles(vector), modes, order, weights, diffusivity)])
    return untiles(out)


def solution(mesh):
    return jax.shard_map(
        body,
        mesh=mesh,
        in_specs=(
            P("mode", None, "space", None),
            P(None, "space", None),
            P("mode", None),
            P(),
            P(),
            P("space", None),
        ),
        out_specs=P("mode", "space", None),
        check_vma=False,
    )
```

```python
import jax
import jax.numpy as jnp
from jax import lax
from jax.experimental import pallas as pl
from jax.experimental.pallas import tpu as pltpu
from jax.sharding import PartitionSpec as P

LEV, NLON, DIFF, MODES, ROWS = 136, 2048, 4, 16, 4
GROUPS = 8
GLEV = LEV // GROUPS
TILES = NLON // 128
CHUNKS = 4
SUB = TILES * ROWS // CHUNKS
WIDE = NLON // CHUNKS
PADDED = NLON + 256
EXT = ROWS + 2 * DIFF
UP = (9, 5, 8, 12)
FAR, NEAR, PAST = 0, 1, 2
MSGS = CHUNKS + 1
BY_DISTANCE = (4, 3, 5, 2, 6, 1, 7)
TINY = 1e-33
F32, BF16, I16 = jnp.float32, jnp.bfloat16, jnp.int16


def split(a):
    hi = a.astype(BF16)
    return hi, (a - hi.astype(F32)).astype(BF16)


def pack(a, top):
    return jnp.round(a * (32767.0 / top)).astype(I16)


def kernel(x_hbm, v_hbm, modes_hbm, order_hbm, weights_hbm, diff_hbm, out_ref,
           order_ref, weights_ref, xs, vs, mine, nu, mall, nuext, phi, plo, spread, pick, fwd, bwd, field, face, loc, lcat,
           hq, hsc, hqr, hscr, xsib, lsib, own, zf, zfr, zn, zp, zr, tf, tfr, tn, tnr, tp, tpr,
           lsem, m_s, m_r, d_s, d_r, hq_s, hq_r, hs_s, hs_r, sb_s, sb_r, xb_s, xb_r,
           z_s, z_r, t_s, t_r):
    me = lax.axis_index("mode")
    place = lax.axis_index("space")
    ring, core = me // 2, me % 2
    has_prev = place > 0
    has_next = place < lax.axis_size("space") - 1
    right = {"mode": ((ring + 1) % 4) * 2 + core}
    left = {"mode": ((ring + 3) % 4) * 2 + core}
    partner = {"mode": ring * 2 + 1 - core}
    before, after = {"space": place - 1}, {"space": place + 1}

    def remote(src, dst, ss, rs, dev):
        return pltpu.make_async_remote_copy(
            src_ref=src, dst_ref=dst, send_sem=ss, recv_sem=rs, device_id=dev,
            device_id_type=pl.DeviceIdType.MESH)

    barrier = pltpu.get_barrier_semaphore()

    def greet(dev):
        pl.semaphore_signal(barrier, inc=1, device_id=dev, device_id_type=pl.DeviceIdType.MESH)

    for j in BY_DISTANCE:
        greet({"mode": (me + j) % GROUPS})
    pl.when(has_prev)(lambda: greet(before))
    pl.when(has_next)(lambda: greet(after))

    def chunk_rows(n):
        return pl.ds(pl.multiple_of(n * SUB, SUB), SUB)

    get_modes = pltpu.make_async_copy(modes_hbm, mine, lsem.at[0])
    get_nu = pltpu.make_async_copy(diff_hbm, nu, lsem.at[1])

    def get_x(n):
        return pltpu.make_async_copy(x_hbm.at[:, chunk_rows(n)], xs.at[:, chunk_rows(n)], lsem.at[2 + n])

    def get_v(n):
        return pltpu.make_async_copy(v_hbm.at[:, chunk_rows(n)], vs.at[:, chunk_rows(n)], lsem.at[2 + CHUNKS + n])

    get_order = pltpu.make_async_copy(order_hbm, order_ref, lsem.at[2 + 2 * CHUNKS])
    get_weights = pltpu.make_async_copy(weights_hbm, weights_ref, lsem.at[3 + 2 * CHUNKS])
    for copy in (get_modes, get_nu, get_order, get_weights):
        copy.start()
    for n in range(CHUNKS):
        get_x(n).start()
        get_v(n).start()

    lane_level = lax.broadcasted_iota(jnp.int32, (256, LEV * 8), 1) >> 3
    spread[...] = jnp.where(lane_level == lax.broadcasted_iota(jnp.int32, (256, LEV * 8), 0), 1.0, 0.0).astype(BF16)
    get_modes.wait()
    mall[0] = mine[...]
    get_nu.wait()
    get_order.wait()
    get_weights.wait()

    def products(n):
        get_x(n).wait()
        get_v(n).wait()

        for b in range(LEV // 8):
            lev = slice(b * 8, b * 8 + 8)
            p = xs[lev, chunk_rows(n), :].astype(F32) * vs[lev, chunk_rows(n), :]
            for h in range(2):
                hi, lo = split(p[:, 8 * h : 8 * h + 8, :].reshape(64, 128))
                phi[n, b * 64 : b * 64 + 64, 128 * h : 128 * h + 128] = hi
                plo[n, b * 64 : b * 64 + 64, 128 * h : 128 * h + 128] = lo

    pl.semaphore_wait(barrier, GROUPS - 1 + has_prev.astype(jnp.int32) + has_next.astype(jnp.int32))

    def send_modes(j):
        return remote(mall.at[0], mall.at[j], m_s.at[j], m_r.at[j], {"mode": (me + j) % GROUPS})

    for j in BY_DISTANCE:
        send_modes(j).start()
    nu_up = remote(nu, nuext.at[0], d_s.at[0], d_r.at[0], after)
    nu_down = remote(nu, nuext.at[1], d_s.at[1], d_r.at[1], before)
    pl.when(has_next)(lambda: nu_up.start())
    pl.when(has_prev)(lambda: nu_down.start())

    def run(stage):
        def step(n, carry):
            stage(n)
            return carry
        lax.fori_loop(0, CHUNKS, step, 0)

    def levels_of(i, c):
        return pl.ds((((ring + i) % 4) * 2 + c) * GLEV, GLEV)

    for i in range(4):
        level = (((ring + i) % 4) * 2 + core) * GLEV + (lax.broadcasted_iota(jnp.int32, (LEV, 256), 0) >> 3)
        pick[i * LEV : (i + 1) * LEV, :] = jnp.where(
            lax.broadcasted_iota(jnp.int32, (LEV, 256), 1) == level, 1.0, 0.0).astype(BF16)

    run(products)

    def lend(i):
        return remote(xs.at[levels_of(i, 1 - core)], xsib.at[i], xb_s.at[i], xb_r.at[i], partner)

    for j in range(1, GROUPS):
        send_modes(j).wait_recv()
    modes = jnp.zeros((MODES, LEV), F32)
    for j in range(GROUPS):
        row = lax.broadcasted_iota(jnp.int32, (MODES, LEV), 0) - 2 * ((me - j + GROUPS) % GROUPS)
        modes = jnp.where(row == 0, mall[j, 0:1, :], jnp.where(row == 1, mall[j, 1:2, :], modes))
    modes = jnp.concatenate([modes, jnp.zeros((MODES, 256 - LEV), F32)], axis=1)
    modes_hi, modes_lo = split(modes)

    both = jnp.dot(jnp.concatenate([modes_hi, modes_lo], axis=0), spread[...], preferred_element_type=F32)
    sub = lax.broadcasted_iota(jnp.int32, (MODES, LEV * 8), 1) & 7
    for half in range(2):
        rows = both[half * MODES : (half + 1) * MODES]
        for q in range(8):
            fwd[half * 128 + q * MODES : half * 128 + (q + 1) * MODES, :] = jnp.where(sub == q, rows, 0.0).astype(BF16)

    def peak(a):
        return jnp.maximum(jnp.max(jnp.max(jnp.abs(a), axis=0), axis=0, keepdims=True), TINY)

    def project(n):
        main = jnp.dot(fwd[...], phi[n], preferred_element_type=F32)
        rest = jnp.dot(fwd[0:128, :], plo[n], preferred_element_type=F32)
        total = main[0:128] + main[128:256] + rest
        for par in range(2):
            for r in range(ROWS):
                for h in range(2):
                    at = (1 + 4 * n + 2 * h + par) * 128
                    q = (par * ROWS + r) * MODES
                    field[DIFF + r, :, at : at + 128] = total[q : q + MODES, h * 128 : h * 128 + 128]

    def halo_lanes(i):
        if isinstance(i, int) and i == 0:
            return pl.ds(0, 256)
        return pl.ds(pl.multiple_of(i * WIDE - WIDE + 256, 128), WIDE)

    def halo(i, way):
        lanes = halo_lanes(i)
        dev = after if way == 0 else before
        return (remote(hq.at[:, :, lanes], hqr.at[way, :, :, lanes], hq_s.at[way, i], hq_r.at[way, i], dev),
                remote(hsc.at[:, lanes], hscr.at[way, :, lanes], hs_s.at[way, i], hs_r.at[way, i], dev))

    def each(copies, what):
        for copy in copies:
            getattr(copy, what)()

    def send_halo(i):
        lanes = halo_lanes(i)
        u = field[DIFF : DIFF + ROWS, :, lanes]
        top = peak(u)
        hsc[:, lanes] = top * (1.0 / 32767.0)
        hq[:, :, lanes] = pack(u, top[None])
        pl.when(has_next)(lambda: each(halo(i, 0), "start"))
        pl.when(has_prev)(lambda: each(halo(i, 1), "start"))

    own_rows = slice(DIFF, DIFF + ROWS)
    project(3)
    field[own_rows, :, 0:128] = field[own_rows, :, NLON : NLON + 128]
    project(0)
    field[own_rows, :, NLON + 128 : PADDED] = field[own_rows, :, 128:256]
    send_halo(0)
    project(1)
    send_halo(1)
    project(2)
    for i in range(2, MSGS):
        send_halo(i)

    for i in range(4):
        lend(i).start()

    rep_hi = jnp.concatenate([modes_hi] * 8, axis=0)
    rep_lo = jnp.concatenate([modes_lo] * 8, axis=0)
    same = (lax.broadcasted_iota(jnp.int32, (4 * LEV, 128), 0) & 7) == (lax.broadcasted_iota(jnp.int32, (4 * LEV, 128), 1) >> 4)
    last = (((1,), (1,)), ((), ()))
    hi = jnp.where(same, lax.dot_general(pick[...], rep_hi, last, preferred_element_type=F32), 0.0).astype(BF16)
    bwd[:, 0:128] = hi
    bwd[:, 128:256] = hi
    lo = lax.dot_general(pick[...], rep_lo, last, preferred_element_type=F32)
    bwd[:, 256:384] = jnp.where(same, lo, 0.0).astype(BF16)

    @pl.when(has_prev)
    def _():
        nu_up.wait_recv()

    @pl.when(has_next)
    def _():
        nu_down.wait_recv()

    @pl.when(jnp.logical_not(has_prev))
    def _():
        nuext[0] = jnp.zeros((ROWS, NLON), F32)
        field[0:DIFF] = jnp.zeros((DIFF, MODES, PADDED), F32)

    @pl.when(jnp.logical_not(has_next))
    def _():
        nuext[1] = jnp.zeros((ROWS, NLON), F32)
        field[DIFF + ROWS : EXT] = jnp.zeros((DIFF, MODES, PADDED), F32)

    def nu_row(a):
        src = nuext[0] if a < DIFF else nu[...] if a < DIFF + ROWS else nuext[1]
        r = a % ROWS
        return jnp.broadcast_to(src[r : r + 1, :], (8, NLON))

    for a in range(EXT - 1):
        here = nu_row(a)
        for c, other in enumerate((pltpu.roll(here, NLON - 1, 1), nu_row(a + 1))):
            arm = 0.5 * (here + other)
            face[c, a, :, 128 : NLON + 128] = arm
            face[c, a, :, 0:128] = arm[:, NLON - 128 : NLON]
            face[c, a, :, NLON + 128 : PADDED] = arm[:, 0:128]

    weight = jnp.float32(0.0)
    for s in range(GROUPS):
        weight = weight + jnp.where(order_ref[s] == me, weights_ref[s], 0.0)

    def take_halo(i):
        lanes = halo_lanes(i)

        @pl.when(has_prev)
        def _():
            each(halo(i, 0), "wait_recv")
            field[0:DIFF, :, lanes] = hqr[0, :, :, lanes].astype(F32) * hscr[0, :, lanes][None]

        @pl.when(has_next)
        def _():
            each(halo(i, 1), "wait_recv")
            field[DIFF + ROWS : EXT, :, lanes] = hqr[1, :, :, lanes].astype(F32) * hscr[1, :, lanes][None]

    window = WIDE + 256
    top_mask, low_mask = has_prev.astype(F32), has_next.astype(F32)

    def diffuse(n):
        lanes = pl.ds(pl.multiple_of(n * WIDE, 128), window)
        for kh in range(2):
            ks = slice(kh * 8, kh * 8 + 8)
            levels = [{} for _ in range(DIFF + 1)]
            souths = [{} for _ in range(DIFF + 1)]

            def cell(s, a):
                return field[a, ks, lanes] if s == 0 else levels[s][a]

            def south_of(s, a):
                if a not in souths[s]:
                    souths[s][a] = face[1, a, :, lanes] * (cell(s, a + 1) - cell(s, a))
                return souths[s][a]

            for t in range(1, EXT + 2 * DIFF):
                for s in range(1, DIFF + 1):
                    a = t - 2 * (s - 1) + (s - 1)
                    if s <= a < EXT - s:
                        c = cell(s - 1, a)
                        east = face[0, a, :, lanes] * (pltpu.roll(c, window - 1, 1) - c)
                        total = c + (south_of(s - 1, a) - south_of(s - 1, a - 1)) + (east - pltpu.roll(east, 1, 1))
                        if a < DIFF:
                            total = total * top_mask
                        elif a >= DIFF + ROWS:
                            total = total * low_mask
                        levels[s][a] = total
            for r in range(ROWS):
                loc[r, ks, :] = weight * levels[DIFF][DIFF + r][:, 128 : 128 + WIDE]
        for par in range(2):
            for r in range(ROWS):
                q = (par * ROWS + r) * MODES
                for h in range(2):
                    t = (2 * h + par) * 128
                    hi, lo = split(loc[r, :, t : t + 128])
                    cols = slice(h * 128, h * 128 + 128)
                    lcat[n, q : q + MODES, cols] = hi
                    lcat[n, 128 + q : 128 + q + MODES, cols] = lo

    def share(n):
        return remote(lcat.at[n], lsib.at[n], sb_s.at[n], sb_r.at[n], partner)

    def backward(terms):
        return (jnp.dot(bwd[:, 0:256], terms[...], preferred_element_type=F32)
                + jnp.dot(bwd[:, 256:384], terms[0:128, :], preferred_element_type=F32))

    def times(back, i, x):
        return jnp.concatenate(
            [x[:, 8 * h : 8 * h + 8, :] * back[i * LEV : (i + 1) * LEV, h * 128 : h * 128 + 128].reshape(GLEV, 8, 128)
             for h in range(2)], axis=1)

    def carry_sum(kind, n, way, c):
        dest = (c + 2) % 4 if kind == FAR else (c + 1) % 4 if way == 0 else (c + 3) % 4
        rising = (way == 0) == (kind != NEAR)
        cut = slice(0, UP[dest]) if rising else slice(UP[dest], GLEV)
        dev = right if way == 0 else left
        if kind == FAR:
            src, dst, one, two = zf.at[n, cut], zfr.at[n, way, cut], tf.at[n], tfr.at[n, way]
        elif kind == NEAR:
            src, dst, one, two = zn.at[n, way, cut], zr.at[n, way, cut], tn.at[n, way], tnr.at[n, way]
        else:
            src, dst, one, two = zp.at[n, way, cut], zr.at[n, way, cut], tp.at[n, way], tpr.at[n, way]
        return (remote(src, dst, z_s.at[kind, way, n], z_r.at[kind, way, n], dev),
                remote(one, two, t_s.at[kind, way, n], t_r.at[kind, way, n], dev))

    def act(kind, n, way, what):
        step = 0 if what != "wait_recv" else 3 if way == 0 else 1
        for c in range(4):
            pl.when(ring == c)(lambda c=c: each(carry_sum(kind, n, way, (c + step) % 4), what))

    lev_index = lax.broadcasted_iota(jnp.int32, (GLEV, 1, 128), 0)

    def rises(step):
        dest = (ring + step) % 4
        up = jnp.int32(UP[0])
        for d in range(1, 4):
            up = jnp.where(dest == d, UP[d], up)
        return lev_index < up

    def quantize(a, q, t):
        top = peak(a)
        t[...] = top * (1.0 / 32767.0)
        q[...] = pack(a, top[None])

    def stage_a(n):
        take_halo(n + 1)
        diffuse(n)
        share(n).start()
        back = backward(lcat.at[n])
        for i in range(4):
            own[n, i] = times(back, i, xs[levels_of(i, core), chunk_rows(n), :].astype(F32))

    def stage_b(n):
        share(n).wait_recv()
        back = backward(lsib.at[n])

        def both(i):
            return own[n, i] + times(back, i, xsib[i, :, chunk_rows(n), :].astype(F32))

        quantize(both(2), zf.at[n], tf.at[n])
        for way in range(2):
            act(FAR, n, way, "start")
        for way in range(2):
            i = 1 if way == 0 else 3
            own[n, i] = both(i)
            quantize(own[n, i], zn.at[n, way], tn.at[n, way])
        pl.when(n < 2)(lambda: start_near(n))
        own[n, 0] = both(0)

    def start_near(n):
        for way in range(2):
            act(NEAR, n, way, "start")

    def stage_c(n):
        for way in range(2):
            act(FAR, n, way, "wait_recv")
            got = own[n, 1 if way == 0 else 3] + zfr[n, way].astype(F32) * tfr[n, way][None]
            up = rises(1 if way == 0 else 3)
            a = jnp.where(up, got, 0.0) if way == 0 else jnp.where(up, 0.0, got)
            quantize(a, zp.at[n, way], tp.at[n, way])
            act(PAST, n, way, "start")

    def stage_d(n):
        total = own[n, 0]
        up = rises(0)
        for way in range(2):
            act(NEAR, n, way, "wait_recv")
            act(PAST, n, way, "wait_recv")
            scale = jnp.where(up if way == 0 else jnp.logical_not(up), tpr[n, way][None], tnr[n, way][None])
            total = total + zr[n, way].astype(F32) * scale
        out_ref[:, chunk_rows(n), :] = total

    take_halo(0)
    for i in range(4):
        lend(i).wait_recv()

    def pipe(it, carry):
        pl.when(it < CHUNKS)(lambda: stage_a(it))
        pl.when(it != 1)(lambda: stage_b(jnp.maximum(it - 1, 0)))
        return carry

    def later_near(n, carry):
        start_near(n)
        return carry

    lax.fori_loop(0, CHUNKS + 1, pipe, 0)
    lax.fori_loop(2, CHUNKS, later_near, 0)
    run(stage_c)
    run(stage_d)

    for j in range(1, GROUPS):
        send_modes(j).wait_send()
    for i in range(4):
        lend(i).wait_send()

    @pl.when(has_next)
    def _():
        nu_up.wait_send()
        for i in range(MSGS):
            each(halo(i, 0), "wait_send")

    @pl.when(has_prev)
    def _():
        nu_down.wait_send()
        for i in range(MSGS):
            each(halo(i, 1), "wait_send")

    def sent(n):
        share(n).wait_send()
        for way in range(2):
            for kind in (FAR, NEAR, PAST):
                act(kind, n, way, "wait_send")

    run(sent)


def tiles(a):
    lev = a.shape[0]
    return a.reshape(lev, ROWS, TILES, 128).transpose(0, 2, 1, 3).reshape(lev, TILES * ROWS, 128)


def untiles(a):
    lev = a.shape[0]
    return a.reshape(lev, TILES, ROWS, 128).transpose(0, 2, 1, 3).reshape(lev, ROWS, NLON)


def body(anomalies, vector, modes, order, weights, diffusivity):
    vmem, dma = pltpu.VMEM, pltpu.SemaphoreType.DMA
    hbm = pl.BlockSpec(memory_space=pltpu.HBM)
    rows = TILES * ROWS
    out = pl.pallas_call(
        kernel,
        out_shape=jax.ShapeDtypeStruct((GLEV, rows, 128), F32),
        in_specs=[hbm] * 6,
        out_specs=pl.BlockSpec(memory_space=pltpu.VMEM),
        scratch_shapes=[
            pltpu.SMEM((GROUPS,), jnp.int32),
            pltpu.SMEM((GROUPS,), F32),
            vmem((LEV, rows, 128), BF16),
            vmem((LEV, rows, 128), F32),
            vmem((2, LEV), F32),
            vmem((ROWS, NLON), F32),
            vmem((GROUPS, 2, LEV), F32),
            vmem((2, ROWS, NLON), F32),
            vmem((CHUNKS, LEV * 8, 256), BF16),
            vmem((CHUNKS, LEV * 8, 256), BF16),
            vmem((256, LEV * 8), BF16),
            vmem((4 * LEV, 256), BF16),
            vmem((256, LEV * 8), BF16),
            vmem((4 * LEV, 384), BF16),
            vmem((EXT, MODES, PADDED), F32),
            vmem((2, EXT - 1, 8, PADDED), F32),
            vmem((ROWS, MODES, WIDE), F32),
            vmem((CHUNKS, 256, 256), BF16),
            vmem((ROWS, MODES, PADDED), I16),
            vmem((1, PADDED), F32),
            vmem((2, ROWS, MODES, PADDED), I16),
            vmem((2, 1, PADDED), F32),
            vmem((4, GLEV, rows, 128), BF16),
            vmem((CHUNKS, 256, 256), BF16),
            vmem((CHUNKS, 4, GLEV, SUB, 128), F32),
            vmem((CHUNKS, GLEV, SUB, 128), I16),
            vmem((CHUNKS, 2, GLEV, SUB, 128), I16),
            vmem((CHUNKS, 2, GLEV, SUB, 128), I16),
            vmem((CHUNKS, 2, GLEV, SUB, 128), I16),
            vmem((CHUNKS, 2, GLEV, SUB, 128), I16),
            vmem((CHUNKS, 1, 128), F32),
            vmem((CHUNKS, 2, 1, 128), F32),
            vmem((CHUNKS, 2, 1, 128), F32),
            vmem((CHUNKS, 2, 1, 128), F32),
            vmem((CHUNKS, 2, 1, 128), F32),
            vmem((CHUNKS, 2, 1, 128), F32),
            dma((4 + 2 * CHUNKS,)),
            dma((GROUPS,)), dma((GROUPS,)), dma((2,)), dma((2,)),
            dma((2, MSGS)), dma((2, MSGS)), dma((2, MSGS)), dma((2, MSGS)),
            dma((CHUNKS,)), dma((CHUNKS,)), dma((4,)), dma((4,)),
            dma((3, 2, CHUNKS)), dma((3, 2, CHUNKS)), dma((3, 2, CHUNKS)), dma((3, 2, CHUNKS)),
        ],
        compiler_params=pltpu.CompilerParams(
            collective_id=0, has_side_effects=True, vmem_limit_bytes=53 * 2**20),
    )(*[pltpu.with_memory_space_constraint(a, pltpu.HBM) for a in (tiles(anomalies[0]), tiles(vector), modes, order, weights, diffusivity)])
    return untiles(out)


def solution(mesh):
    return jax.shard_map(
        body,
        mesh=mesh,
        in_specs=(
            P("mode", None, "space", None),
            P(None, "space", None),
            P("mode", None),
            P(),
            P(),
            P("space", None),
        ),
        out_specs=P("mode", "space", None),
        check_vma=False,
    )
```
